32 devices in a mesh: dp: 8 (over y, x, core), tensor: 4 (over z).
Axes of the slice: x: 2, y: 2, z: 4, core: 2. Of those that a mesh axis runs over, the one named last changes fastest.
Arguments:
- tokens: float32 [4864, 1024], P(('dp', 'tensor')), may hold values from -6 to 6
- counts: int32 [8], P('dp'), may hold values from 457 to 577, as said below
- vectors: float32 [8, 1024], P(None, ('dp', 'tensor')), may hold values from -2 to 3, as said below
- fc1_bias: float32 [4096], P(('dp', 'tensor')), may hold values from -4 to 4
- w_qkv: bfloat16 [3, 1024, 1024], P(None, 'dp', 'tensor'), may hold values from -0.1875 to 0.1875
- w_out: bfloat16 [1024, 1024], P('tensor', 'dp'), may hold values from -2.5 to 2.5
- w_fc1: bfloat16 [1024, 4096], P('dp', 'tensor'), may hold values from -0.1875 to 0.1875
- w_fc2: bfloat16 [4096, 1024], P('tensor', 'dp'), may hold values from -0.09375 to 0.09375
- cotangent: float32 [4864, 1024], P(('dp', 'tensor')), may hold values from -6 to 6
Outputs:
- layer_out: float32 [4864, 1024], P(('dp', 'tensor'))
- input_grad: float32 [4864, 1024], P(('dp', 'tensor'))
- vectors_grad: float32 [8, 1024], P(None, ('dp', 'tensor'))
- fc1_bias_grad: float32 [4096], P(('dp', 'tensor'))
- qkv_grad: float32 [3, 1024, 1024], P(None, 'dp', 'tensor')
- out_grad: float32 [1024, 1024], P('tensor', 'dp')
- fc1_grad: float32 [1024, 4096], P('dp', 'tensor')
- fc2_grad: float32 [4096, 1024], P('tensor', 'dp')
The draws below stay inside these ranges and needn't reach their ends.
Inputs may be any that keep to these rules, and one draw needn't show every extreme that they name: `counts`: an image's valid tokens are its first ones; some image has exactly 577. `vectors`: rows 0 and 5 are gains near 1; the other rows are biases.
All inputs are finite; a program needn't handle non-finite values.
Results may differ from the reference program's by a relative error of at most 0.017.
Values may be sent and summed in bfloat16 or wider, within the bound.
A program may use at most 128 MiB of HBM per device.

```python
import jax
import jax.numpy as jnp
from jax import lax

D = 1024
HEADS = 16
HEAD_DIM = 64
FF = 4096
LEN = 577
SEQ = 608
FEWEST = 457
IMAGES = 8
TOKENS = 4864


def draw_counts(key, part):
    key = jax.random.fold_in(key, 11)
    first, second = jax.random.split(key)
    drawn = jax.random.randint(first, (IMAGES,), FEWEST, LEN + 1, dtype=jnp.int32)
    chosen = jax.random.randint(second, (), 0, IMAGES, dtype=jnp.int32)
    return jnp.where(jnp.arange(IMAGES, dtype=jnp.int32) == chosen, LEN, drawn).astype(jnp.int32)


def draw_vectors(key, part):
    key = jax.random.fold_in(key, 23)
    noise = jnp.clip(jax.random.normal(key, (8, D), jnp.float32), -6.0, 6.0)
    row_number = jnp.arange(8, dtype=jnp.int32)[:, None]
    is_gain = (row_number == 0) | (row_number == 5)
    return jnp.where(is_gain, 1.0 + 0.15 * noise, 0.3 * noise).astype(jnp.float32)


def strengthened(array, key, source, target, blocks, factor):
    owner, partner = [(jnp.arange(array.shape[axis_at]) // (array.shape[axis_at] // blocks)).reshape([-1 if axis == axis_at else 1 for axis in range(array.ndim)]) for axis_at in (source, target)]
    chosen = jax.random.permutation(key, blocks)[partner]
    strong = (owner == chosen) | (owner == (partner + blocks // 2) % blocks)
    return jnp.where(strong, factor * array, array)


def block_levels(own_key, extent, shards, low, high):
    factor_of = 1.0
    for position, blocks in shards:
        steps = jax.random.uniform(jax.random.fold_in(jax.random.fold_in(own_key, 6), position), (blocks,), jnp.float32, low / len(shards), high / len(shards))
        factor_of = factor_of * jnp.repeat(jnp.exp(steps), extent[position] // blocks).reshape((-1,) + (1,) * (len(extent) - 1 - position))
    return factor_of


def normal_values(own_key, shape, width, reach, shards=(), kind=jnp.bfloat16):
    level = block_levels(own_key, shape, shards, -0.22, 0.18) if shards else 1.0
    array = jax.random.normal(own_key, shape, jnp.float32) * width * level
    return jnp.minimum(jnp.maximum(array, -reach), reach).astype(kind)


def gaussian_with(key, extent, width, bound, pieces, heavy, kind=jnp.bfloat16):
    result = width * jax.random.normal(key, extent, jnp.float32)
    if pieces:
        result = result * block_levels(key, extent, pieces, -0.22, 0.18)
    return jnp.clip(strengthened(result, jax.random.fold_in(key, 3), *heavy), -bound, bound).astype(kind)


def setup_inputs(seed: int = 0) -> dict:
    splits = jax.random.split(jax.random.key(seed), 10)
    tokens = gaussian_with(splits[0], (TOKENS, D), 1.0, 6.0, ((0, 32),), (0, 1, 32, 2.75), jnp.float32)
    counts = draw_counts(jax.random.fold_in(splits[9], 71), 0)
    vectors = draw_vectors(jax.random.fold_in(splits[9], 71), 0)
    fc1_bias = normal_values(splits[3], (FF,), 0.3, 4.0, ((0, 32),), jnp.float32)
    w_qkv = normal_values(splits[4], (3, D, D), D ** -0.5, 0.1875, ((1, 8), (2, 4)))
    w_out = normal_values(splits[5], (D, D), (max(4 * D // SEQ, 1)) ** -0.5, 2.5, ((0, 4), (1, 8)))
    w_fc1 = normal_values(splits[6], (D, FF), D ** -0.5, 0.1875, ((0, 8), (1, 4)))
    w_fc2 = normal_values(splits[7], (FF, D), FF ** -0.5, 0.09375, ((0, 4), (1, 8)))
    cotangent = gaussian_with(splits[8], (TOKENS, D), 1.0, 6.0, ((0, 32),), (0, 1, 32, 2.75), jnp.float32)
    return dict(tokens=tokens, counts=counts, vectors=vectors, fc1_bias=fc1_bias, w_qkv=w_qkv, w_out=w_out, w_fc1=w_fc1, w_fc2=w_fc2, cotangent=cotangent)


@jax.custom_vjp
def low(v):
    return lax.optimization_barrier(v.astype(jnp.bfloat16)).astype(jnp.float32)

@jax.custom_vjp
def low_back(v):
    return v

def low_keep(v):
    return (low(v), None)

def low_pass(kept, grad):
    return (grad,)

def back_keep(v):
    return (v, None)

def back_low(kept, grad):
    return (low(grad),)
low.defvjp(low_keep, low_pass)
low_back.defvjp(back_keep, back_low)
EPSILON = 1e-06
NEGATIVE = -1e+30

def precise(left, right):
    return jnp.dot(left, right, precision=lax.Precision.HIGHEST)

def layer_norm(values, gain, shift):
    centred = values - lax.optimization_barrier(jnp.mean(values, axis=-1, keepdims=True))
    spread = lax.optimization_barrier(jnp.mean(centred * centred, axis=-1, keepdims=True))
    return centred * lax.rsqrt(spread + EPSILON) * gain + shift

def one_image(weights, rows, count):
    vectors, fc1_bias, w_qkv, w_out, w_fc1, w_fc2 = weights
    place = jnp.arange(SEQ, dtype=jnp.int32)
    valid = (place < count).astype(jnp.float32)[:, None]
    normed = low(layer_norm(rows, vectors[0], vectors[1]))
    query = low(low_back(precise(normed, w_qkv[0]) + vectors[2])).reshape(SEQ, HEADS, HEAD_DIM)
    keys = low(low_back(precise(normed, w_qkv[1]))).reshape(SEQ, HEADS, HEAD_DIM)
    values = low(low_back(precise(normed, w_qkv[2]) + vectors[3])).reshape(SEQ, HEADS, HEAD_DIM)
    scores = jnp.einsum('qhd,khd->hqk', query, keys, precision=lax.Precision.HIGHEST) * HEAD_DIM ** (-0.5)
    scores = low_back(scores)
    scores = jnp.where((place < count)[None, None, :], scores, NEGATIVE)
    largest = lax.optimization_barrier(jnp.max(scores, axis=-1, keepdims=True))
    powers = jnp.exp(scores - largest)
    probs = low(powers / lax.optimization_barrier(jnp.sum(powers, axis=-1, keepdims=True)))
    mixed = jnp.einsum('hqk,khd->qhd', probs, values, precision=lax.Precision.HIGHEST)
    mixed = low(low_back(mixed)).reshape(SEQ, D)
    branch = low_back(precise(mixed, w_out))
    middle = rows + valid * (branch + vectors[4])
    normed2 = low(layer_norm(middle, vectors[5], vectors[6]))
    pre = low_back(precise(normed2, w_fc1) + fc1_bias)
    hidden = low(jax.nn.gelu(pre, approximate=False))
    feed = low_back(precise(hidden, w_fc2))
    return middle + valid * (feed + vectors[7])

def forward(tokens, vectors, fc1_bias, w_qkv, w_out, w_fc1, w_fc2, counts):
    weights = (vectors, fc1_bias, w_qkv, w_out, w_fc1, w_fc2)

    def one_entry(entry):
        return one_image(weights, entry[0], entry[1])
    results = lax.map(jax.checkpoint(one_entry), (tokens.reshape(IMAGES, SEQ, D), counts))
    return results.reshape(TOKENS, D)

def reference(tokens, counts, vectors, fc1_bias, w_qkv, w_out, w_fc1, w_fc2, cotangent):
    operands = (tokens.astype(jnp.float32), vectors.astype(jnp.float32), fc1_bias.astype(jnp.float32), w_qkv.astype(jnp.float32), w_out.astype(jnp.float32), w_fc1.astype(jnp.float32), w_fc2.astype(jnp.float32))

    def applied(tok, vec, fbias, wqkv, wout, wfc1, wfc2):
        return forward(tok, vec, fbias, wqkv, wout, wfc1, wfc2, counts)
    layer_out, backward = jax.vjp(applied, *operands)
    grads = backward(cotangent.astype(jnp.float32))
    return (layer_out, grads[0], grads[1], grads[2], grads[3], grads[4], grads[5], grads[6])
```

```python
import functools

import jax
import jax.numpy as jnp
from jax import lax
from jax.experimental import pallas as pl
from jax.experimental.pallas import tpu as pltpu
from jax.sharding import PartitionSpec as P

HEAD_DIM = 64


EPSILON = 1e-06
NEGATIVE = -1e30
MESH = pl.DeviceIdType.MESH
LANES = 128


def peer_at(axis, k):
    if axis == "all":
        dp, tensor = lax.axis_size("dp"), lax.axis_size("tensor")
        index = lax.rem(lax.axis_index("dp") * tensor + lax.axis_index("tensor") + k, dp * tensor)
        return index, {"dp": index // tensor, "tensor": lax.rem(index, tensor)}
    index = lax.rem(lax.axis_index(axis) + k, lax.axis_size(axis))
    return index, {axis: index}


def my_index(axis):
    if axis == "all":
        return lax.axis_index("dp") * lax.axis_size("tensor") + lax.axis_index("tensor")
    return lax.axis_index(axis)


def size_of(axis):
    if axis == "all":
        return lax.axis_size("dp") * lax.axis_size("tensor")
    return lax.axis_size(axis)


def view(ref, spot, index):
    if spot is None:
        return ref.at[index]
    dim, width = spot
    place = pl.ds(pl.multiple_of(index * width, width), width)
    return ref.at[tuple([slice(None)] * dim + [place])]


def for_each(count, body):
    lax.fori_loop(0, count, lambda k, carry: (body(k), carry)[1], 0)


class Gather:
    def __init__(self, axis, block, spot=None):
        self.axis, self.array, self.spot = axis, block, spot
        shape = list(block.shape)
        if spot is None:
            shape = [size_of(axis)] + shape
        else:
            shape[spot[0]] *= size_of(axis)
        self.out = jax.ShapeDtypeStruct(tuple(shape), block.dtype)
        self.sems = [
            pltpu.SemaphoreType.DMA((size_of(axis),)),
            pltpu.SemaphoreType.DMA((size_of(axis),)),
            pltpu.SemaphoreType.DMA,
        ]

    def own(self, src, out, sems):
        return pltpu.make_async_copy(src, view(out, self.spot, my_index(self.axis)), sems[2])

    def copy(self, src, out, sems, k):
        _, device = peer_at(self.axis, k)
        mine = view(out, self.spot, my_index(self.axis))
        return pltpu.make_async_remote_copy(
            src, mine, sems[0].at[k], sems[1].at[k], device_id=device, device_id_type=MESH
        )

    def start(self, src, out, sems):
        for_each(size_of(self.axis) - 1, lambda k: self.copy(src, out, sems, k + 1).start())
        self.own(src, out, sems).start()

    def middle(self, src, out, sems):
        pass

    def finish(self, src, out, sems):
        for_each(size_of(self.axis) - 1, lambda k: self.copy(src, out, sems, k + 1).wait())
        self.own(src, out, sems).wait()


class PairGather(Gather):
    def __init__(self, block, spot=None):
        super().__init__("dp", block, spot)
        half = size_of("dp") // 2
        self.sems = [pltpu.SemaphoreType.DMA((half,)) for _ in range(4)]
        self.sems.append(pltpu.SemaphoreType.DMA)

    def own(self, src, out, sems):
        return pltpu.make_async_copy(src, view(out, self.spot, my_index("dp")), sems[4])

    def away(self, src, out, sems, k):
        _, device = peer_at("dp", 2 * k)
        mine = view(out, self.spot, my_index("dp"))
        return pltpu.make_async_remote_copy(
            src, mine, sems[0].at[k], sems[1].at[k], device_id=device, device_id_type=MESH
        )

    def share(self, src, out, sems, k, first=False):
        count = size_of("dp")
        me = my_index("dp")
        place = view(out, self.spot, lax.rem(me - 2 * k + count, count))
        return pltpu.make_async_remote_copy(
            src if first else place,
            place,
            sems[2].at[k],
            sems[3].at[k],
            device_id={"dp": me + 1 - 2 * lax.rem(me, 2)},
            device_id_type=MESH,
        )

    def start(self, src, out, sems):
        for_each(size_of("dp") // 2 - 1, lambda k: self.away(src, out, sems, k + 1).start())
        self.share(src, out, sems, 0, True).start()
        self.own(src, out, sems).start()

    def middle(self, src, out, sems):
        def pass_on(k):
            self.away(src, out, sems, k + 1).wait_recv()
            self.share(src, out, sems, k + 1).start()

        for_each(size_of("dp") // 2 - 1, pass_on)

    def finish(self, src, out, sems):
        for_each(size_of("dp") // 2 - 1, lambda k: self.away(src, out, sems, k + 1).wait_send())
        self.share(src, out, sems, 0, True).wait()
        for_each(size_of("dp") // 2 - 1, lambda k: self.share(src, out, sems, k + 1).wait())
        self.own(src, out, sems).wait()


class Swap:
    def __init__(self, axis, array, spot=None):
        self.axis, self.array, self.spot = axis, array, spot
        shape = list(array.shape)
        if spot is None:
            shape = shape[1:]
        else:
            shape[spot[0]] = spot[1]
        self.out = jax.ShapeDtypeStruct((size_of(axis) - 1, *shape), array.dtype)
        self.sems = [pltpu.SemaphoreType.DMA((size_of(axis),)) for _ in range(2)]

    def copy(self, src, out, sems, k):
        index, device = peer_at(self.axis, k)
        return pltpu.make_async_remote_copy(
            view(src, self.spot, index),
            out.at[k - 1],
            sems[0].at[k],
            sems[1].at[k],
            device_id=device,
            device_id_type=MESH,
        )

    def start(self, src, out, sems):
        for_each(size_of(self.axis) - 1, lambda k: self.copy(src, out, sems, k + 1).start())

    def middle(self, src, out, sems):
        pass

    def finish(self, src, out, sems):
        for_each(size_of(self.axis) - 1, lambda k: self.copy(src, out, sems, k + 1).wait())


def exchange(number, *tasks):
    axes = sorted({task.axis for task in tasks})
    if "all" in axes:
        axes = ["all"]
    count = len(tasks)

    def kernel(*refs):
        sources, outs, sems = refs[:count], refs[count : 2 * count], list(refs[2 * count :])
        grouped = []
        for task in tasks:
            grouped.append([sems.pop(0) for _ in task.sems])
        barrier = pltpu.get_barrier_semaphore()

        def greet(axis, k):
            _, device = peer_at(axis, k)
            pl.semaphore_signal(barrier, inc=1, device_id=device, device_id_type=MESH)

        for axis in axes:
            for_each(size_of(axis) - 1, functools.partial(lambda a, k: greet(a, k + 1), axis))
        pl.semaphore_wait(barrier, sum(size_of(axis) - 1 for axis in axes))
        for step in ("start", "middle", "finish"):
            for task, src, out, own in zip(tasks, sources, outs, grouped):
                getattr(task, step)(src, out, own)

    return pl.pallas_call(
        kernel,
        out_shape=[task.out for task in tasks],
        in_specs=[pl.BlockSpec(memory_space=pl.ANY)] * count,
        out_specs=[pl.BlockSpec(memory_space=pl.ANY)] * count,
        scratch_shapes=[sem for task in tasks for sem in task.sems],
        compiler_params=pltpu.CompilerParams(collective_id=number, has_side_effects=True),
    )(*[task.array for task in tasks])


def spot_of(block, dim, width):
    grain = LANES if dim == block.ndim - 1 else 16
    return (dim, width) if width % grain == 0 else None


def weight_gather(block, dim):
    return PairGather(block, spot_of(block, dim, block.shape[dim]))


def joined(gathered, block, dim):
    if gathered.ndim == block.ndim:
        return gathered
    moved = jnp.moveaxis(gathered, 0, dim)
    shape = list(block.shape)
    shape[dim] *= gathered.shape[0]
    return moved.reshape(shape)


def grad_swap(term, dim):
    count = size_of("dp")
    width = term.shape[dim] // count
    low = term.astype(jnp.bfloat16)
    spot = spot_of(low, dim, width)
    if spot is None:
        shape = list(low.shape)
        shape[dim : dim + 1] = [count, width]
        low = jnp.moveaxis(low.reshape(shape), dim, 0)
    return Swap("dp", low, spot)


def own_part(term, axis, dim):
    width = term.shape[dim] // size_of(axis)
    return lax.dynamic_slice_in_dim(term, my_index(axis) * width, width, dim)


def summed(own, others):
    return own + jnp.sum(others.astype(jnp.float32), axis=0)


def layer_norm(values, gain, shift):
    centred = values - jnp.mean(values, axis=-1, keepdims=True)
    spread = jnp.mean(centred * centred, axis=-1, keepdims=True)
    return centred * lax.rsqrt(spread + EPSILON) * gain + shift


def exact_gelu(values):
    return jax.nn.gelu(values, approximate=False)


def masked_scores(query, keys, valid_keys, scale):
    scores = jnp.einsum("qhd,khd->hqk", query, keys, preferred_element_type=jnp.float32) * scale
    return jnp.where(valid_keys[None, None, :], scores, NEGATIVE)


def attend(query, keys, values, valid_keys, scale):
    scores = masked_scores(query, keys, valid_keys, scale)
    largest = jnp.max(scores, axis=-1, keepdims=True)
    powers = jnp.exp(scores - largest)
    total = jnp.sum(powers, axis=-1, keepdims=True)
    probs = (powers / total).astype(jnp.bfloat16)
    mixed = jnp.einsum("hqk,khd->qhd", probs, values, preferred_element_type=jnp.float32)
    return (mixed, largest + jnp.log(total))


def attend_back(query, keys, values, valid_keys, scale, log_total, grad_mixed):
    scores = masked_scores(query, keys, valid_keys, scale)
    probs = jnp.exp(scores - log_total)
    grad_probs = jnp.einsum("qhd,khd->hqk", grad_mixed, values, preferred_element_type=jnp.float32)
    inner = jnp.sum(grad_probs * probs, axis=-1, keepdims=True)
    grad_scores = (probs * (grad_probs - inner)).astype(jnp.bfloat16)
    grad_values = jnp.einsum(
        "hqk,qhd->khd", probs.astype(jnp.bfloat16), grad_mixed, preferred_element_type=jnp.float32
    )
    grad_query = (
        jnp.einsum("hqk,khd->qhd", grad_scores, keys, preferred_element_type=jnp.float32) * scale
    )
    grad_keys = (
        jnp.einsum("hqk,qhd->khd", grad_scores, query, preferred_element_type=jnp.float32) * scale
    )
    return (grad_query, grad_keys, grad_values)


def row_validity(counts, seq, rows):
    places = jnp.arange(rows, dtype=jnp.int32)
    owner = places // seq
    position = places - owner * seq
    picks = owner[:, None] == jnp.arange(counts.shape[0], dtype=jnp.int32)[None, :]
    return position < jnp.sum(jnp.where(picks, counts[None, :], 0), axis=1)


def row_swap(part, rows):
    return Swap("tensor", part.astype(jnp.bfloat16).reshape(-1, rows, part.shape[1]))


def on_device(tokens, counts, vectors, fc1_bias, w_qkv, w_out, w_fc1, w_fc2, cotangent):
    tensor_count = lax.axis_size("tensor")
    tensor_index = lax.axis_index("tensor")
    devices = size_of("all")
    model_width = tokens.shape[1]
    vector_size = vectors.size
    small_size = vector_size + fc1_bias.size
    small_rows = -(-small_size // (8 * LANES)) * 8
    small = jnp.concatenate([vectors.reshape(-1), fc1_bias])
    small = jnp.pad(small, (0, small_rows * LANES - small_size)).reshape(small_rows, LANES)
    local_rows = tokens.shape[0]
    block_rows = local_rows * tensor_count
    images = counts.shape[0]
    local_valid = row_validity(counts, block_rows // images, block_rows)
    local_valid = lax.dynamic_slice_in_dim(local_valid, tensor_index * local_rows, local_rows)
    local_valid = local_valid.astype(jnp.float32)[:, None]
    masked_out = local_valid * cotangent
    small_all, gathered_grad, qkv_all, out_all = exchange(
        0,
        Gather("all", small),
        Gather("tensor", masked_out.astype(jnp.bfloat16)),
        weight_gather(w_qkv, 1),
        weight_gather(w_out, 1),
    )
    qkv_all = joined(qkv_all, w_qkv, 1)
    out_all = joined(out_all, w_out, 1)
    gathered_grad = gathered_grad.reshape(block_rows, model_width)
    small_all = small_all.reshape(devices, small_rows * LANES)
    full_vectors = small_all[:, :vector_size].reshape(devices, vectors.shape[0], -1)
    full_vectors = full_vectors.transpose(1, 0, 2).reshape(vectors.shape[0], model_width)
    full_fc1 = small_all[:, vector_size:small_size].reshape(-1)
    normed = layer_norm(tokens, full_vectors[0], full_vectors[1]).astype(jnp.bfloat16)
    gathered, fc1_all, fc2_all = exchange(
        1, Gather("tensor", normed), weight_gather(w_fc1, 0), weight_gather(w_fc2, 1)
    )
    gathered = gathered.reshape(block_rows, model_width)
    fc1_all = joined(fc1_all, w_fc1, 0)
    fc2_all = joined(fc2_all, w_fc2, 1)
    seq = block_rows // images
    width = qkv_all.shape[2]
    hidden_width = fc1_all.shape[1]
    heads_local = width // HEAD_DIM
    scale = HEAD_DIM ** (-0.5)
    block_valid = row_validity(counts, seq, block_rows)
    query_bias = lax.dynamic_slice_in_dim(full_vectors[2], tensor_index * width, width)
    value_bias = lax.dynamic_slice_in_dim(full_vectors[3], tensor_index * width, width)
    hidden_bias = lax.dynamic_slice_in_dim(full_fc1, tensor_index * hidden_width, hidden_width)
    projected = jnp.einsum("rd,kde->kre", gathered, qkv_all, preferred_element_type=jnp.float32)
    query = (
        (projected[0] + query_bias).astype(jnp.bfloat16).reshape(block_rows, heads_local, HEAD_DIM)
    )
    keys = projected[1].astype(jnp.bfloat16).reshape(block_rows, heads_local, HEAD_DIM)
    values = (
        (projected[2] + value_bias).astype(jnp.bfloat16).reshape(block_rows, heads_local, HEAD_DIM)
    )
    mixed_one, total_one = attend(query, keys, values, block_valid, scale)
    mixed_all = mixed_one.reshape(block_rows, width).astype(jnp.bfloat16)
    attn_part = jnp.dot(mixed_all, out_all, preferred_element_type=jnp.float32)
    (attn_others,) = exchange(2, row_swap(attn_part, local_rows))
    attn_local = summed(own_part(attn_part, "tensor", 0), attn_others)
    middle = tokens + local_valid * (attn_local + full_vectors[4])
    normed2 = layer_norm(middle, full_vectors[5], full_vectors[6]).astype(jnp.bfloat16)
    (gathered2,) = exchange(3, Gather("tensor", normed2))
    gathered2 = gathered2.reshape(block_rows, model_width)
    pre = jnp.dot(gathered2, fc1_all, preferred_element_type=jnp.float32) + hidden_bias
    hidden_float, gelu_back = jax.vjp(exact_gelu, pre)
    hidden = hidden_float.astype(jnp.bfloat16)
    mlp_part = jnp.dot(hidden, fc2_all, preferred_element_type=jnp.float32)
    grad_shift2 = jnp.sum(masked_out, axis=0)
    fc2_term = jnp.einsum("rf,rd->fd", hidden, gathered_grad, preferred_element_type=jnp.float32)
    grad_hidden = jnp.einsum(
        "rd,fd->rf", gathered_grad, fc2_all, preferred_element_type=jnp.float32
    )
    grad_pre = gelu_back(grad_hidden)[0].astype(jnp.bfloat16)
    hidden_bias_grad = jnp.sum(grad_pre.astype(jnp.float32), axis=0)
    fc1_term = jnp.einsum("rd,rf->df", gathered2, grad_pre, preferred_element_type=jnp.float32)
    normed2_part = jnp.einsum("rf,df->rd", grad_pre, fc1_all, preferred_element_type=jnp.float32)
    normed2_others, mlp_others, fc1_others, fc2_others = exchange(
        4,
        row_swap(normed2_part, local_rows),
        row_swap(mlp_part, local_rows),
        grad_swap(fc1_term, 0),
        grad_swap(fc2_term, 1),
    )
    grad_normed2 = summed(own_part(normed2_part, "tensor", 0), normed2_others)
    mlp_local = summed(own_part(mlp_part, "tensor", 0), mlp_others)
    layer_out = middle + local_valid * (mlp_local + full_vectors[7])
    fc1_grad = summed(own_part(fc1_term, "dp", 0), fc1_others)
    fc2_grad = summed(own_part(fc2_term, "dp", 1), fc2_others)
    second_norm, second_back = jax.vjp(layer_norm, middle, full_vectors[5], full_vectors[6])
    grad_through, gain2_grad, shift2_grad = second_back(grad_normed2)
    grad_middle = cotangent + grad_through
    masked_middle = local_valid * grad_middle
    out_bias_grad = jnp.sum(masked_middle, axis=0)
    (gathered_attn,) = exchange(5, Gather("tensor", masked_middle.astype(jnp.bfloat16)))
    gathered_attn = gathered_attn.reshape(block_rows, model_width)
    out_term = jnp.einsum("re,rd->ed", mixed_all, gathered_attn, preferred_element_type=jnp.float32)
    grad_mixed = jnp.einsum("rd,ed->re", gathered_attn, out_all, preferred_element_type=jnp.float32)
    grad_mixed = grad_mixed.astype(jnp.bfloat16).reshape(block_rows, heads_local, HEAD_DIM)
    grad_q, grad_k, grad_v = attend_back(
        query, keys, values, block_valid, scale, total_one, grad_mixed
    )
    grad_query = grad_q.reshape(block_rows, width).astype(jnp.bfloat16)
    grad_keys = grad_k.reshape(block_rows, width).astype(jnp.bfloat16)
    grad_values = grad_v.reshape(block_rows, width).astype(jnp.bfloat16)
    stacked = jnp.stack([grad_query, grad_keys, grad_values])
    query_bias_grad = jnp.sum(grad_query.astype(jnp.float32), axis=0)
    value_bias_grad = jnp.sum(grad_values.astype(jnp.float32), axis=0)
    qkv_term = jnp.einsum("rd,kre->kde", gathered, stacked, preferred_element_type=jnp.float32)
    normed_part = jnp.einsum("kre,kde->rd", stacked, qkv_all, preferred_element_type=jnp.float32)
    normed_others, qkv_others, out_others = exchange(
        6, row_swap(normed_part, local_rows), grad_swap(qkv_term, 1), grad_swap(out_term, 1)
    )
    grad_normed = summed(own_part(normed_part, "tensor", 0), normed_others)
    qkv_grad = summed(own_part(qkv_term, "dp", 1), qkv_others)
    out_grad = summed(own_part(out_term, "dp", 1), out_others)
    first_norm, first_back = jax.vjp(layer_norm, tokens, full_vectors[0], full_vectors[1])
    grad_input_norm, gain1_grad, shift1_grad = first_back(grad_normed)
    input_grad = grad_middle + grad_input_norm
    zeros_model = jnp.zeros((model_width,), jnp.float32)
    query_bias_full = lax.dynamic_update_slice_in_dim(
        zeros_model, query_bias_grad, tensor_index * width, 0
    )
    value_bias_full = lax.dynamic_update_slice_in_dim(
        zeros_model, value_bias_grad, tensor_index * width, 0
    )
    vector_terms = jnp.stack(
        [
            gain1_grad,
            shift1_grad,
            query_bias_full,
            value_bias_full,
            out_bias_grad,
            gain2_grad,
            shift2_grad,
            grad_shift2,
        ]
    )
    zeros_hidden = jnp.zeros((full_fc1.shape[0],), jnp.float32)
    hidden_bias_full = lax.dynamic_update_slice_in_dim(
        zeros_hidden, hidden_bias_grad, tensor_index * hidden_width, 0
    )
    vector_blocks = vector_terms.reshape(vectors.shape[0], devices, -1).transpose(1, 0, 2)
    small_terms = jnp.concatenate(
        [vector_blocks.reshape(devices, -1), hidden_bias_full.reshape(devices, -1)], axis=1
    )
    small_terms = jnp.pad(small_terms, ((0, 0), (0, small_rows * LANES - small_size)))
    small_terms = small_terms.reshape(devices, small_rows, LANES)
    (small_others,) = exchange(7, Swap("all", small_terms))
    small_grad = summed(own_part(small_terms, "all", 0)[0], small_others).reshape(-1)
    vectors_grad = small_grad[:vector_size].reshape(vectors.shape)
    fc1_bias_grad = small_grad[vector_size:small_size]
    return (
        layer_out,
        input_grad,
        vectors_grad,
        fc1_bias_grad,
        qkv_grad,
        out_grad,
        fc1_grad,
        fc2_grad,
    )


def solution(mesh):
    placed = (
        P(("dp", "tensor"), None),
        P("dp"),
        P(None, ("dp", "tensor")),
        P(("dp", "tensor")),
        P(None, "dp", "tensor"),
        P("tensor", "dp"),
        P("dp", "tensor"),
        P("tensor", "dp"),
        P(("dp", "tensor"), None),
    )
    return jax.shard_map(
        on_device,
        mesh=mesh,
        in_specs=placed,
        out_specs=(
            P(("dp", "tensor"), None),
            P(("dp", "tensor"), None),
            P(None, ("dp", "tensor")),
            P(("dp", "tensor")),
            P(None, "dp", "tensor"),
            P("tensor", "dp"),
            P("dp", "tensor"),
            P("tensor", "dp"),
        ),
        check_vma=False,
    )
```

```python
import functools

import jax
import jax.numpy as jnp
from jax import lax
from jax.experimental import pallas as pl
from jax.experimental.pallas import tpu as pltpu
from jax.sharding import PartitionSpec as P

HEAD_DIM = 64


EPSILON = 1e-06
NEGATIVE = -1e30
MESH = pl.DeviceIdType.MESH
LANES = 128


def peer_at(axis, k):
    if axis == "all":
        dp, tensor = lax.axis_size("dp"), lax.axis_size("tensor")
        index = lax.rem(lax.axis_index("dp") * tensor + lax.axis_index("tensor") + k, dp * tensor)
        return index, {"dp": index // tensor, "tensor": lax.rem(index, tensor)}
    index = lax.rem(lax.axis_index(axis) + k, lax.axis_size(axis))
    return index, {axis: index}


def my_index(axis):
    if axis == "all":
        return lax.axis_index("dp") * lax.axis_size("tensor") + lax.axis_index("tensor")
    return lax.axis_index(axis)


def size_of(axis):
    if axis == "all":
        return lax.axis_size("dp") * lax.axis_size("tensor")
    return lax.axis_size(axis)


def view(ref, spot, index):
    if spot is None:
        return ref.at[index]
    dim, width = spot
    place = pl.ds(pl.multiple_of(index * width, width), width)
    return ref.at[tuple([slice(None)] * dim + [place])]


def for_each(count, body):
    lax.fori_loop(0, count, lambda k, carry: (body(k), carry)[1], 0)


class Task:
    place = pl.ANY

    def step(self, number, src, out, sems):
        pass


class Gather(Task):
    def __init__(self, axis, block, spot=None):
        self.axis, self.array, self.spot = axis, block, spot
        shape = list(block.shape)
        if spot is None:
            shape = [size_of(axis)] + shape
        else:
            shape[spot[0]] *= size_of(axis)
        self.out = jax.ShapeDtypeStruct(tuple(shape), block.dtype)
        self.sems = [
            pltpu.SemaphoreType.DMA((size_of(axis),)),
            pltpu.SemaphoreType.DMA((size_of(axis),)),
            pltpu.SemaphoreType.DMA,
        ]

    def own(self, src, out, sems):
        return pltpu.make_async_copy(src, view(out, self.spot, my_index(self.axis)), sems[2])

    def copy(self, src, out, sems, k):
        _, device = peer_at(self.axis, k)
        mine = view(out, self.spot, my_index(self.axis))
        return pltpu.make_async_remote_copy(
            src, mine, sems[0].at[k], sems[1].at[k], device_id=device, device_id_type=MESH
        )

    def start(self, src, out, sems):
        for_each(size_of(self.axis) - 1, lambda k: self.copy(src, out, sems, k + 1).start())
        self.own(src, out, sems).start()

    def finish(self, src, out, sems):
        for_each(size_of(self.axis) - 1, lambda k: self.copy(src, out, sems, k + 1).wait())
        self.own(src, out, sems).wait()


class PairGather(Gather):
    def __init__(self, block, spot=None):
        super().__init__("dp", block, spot)
        half = size_of("dp") // 2
        self.sems = [pltpu.SemaphoreType.DMA((half,)) for _ in range(4)]
        self.sems.append(pltpu.SemaphoreType.DMA)

    def own(self, src, out, sems):
        return pltpu.make_async_copy(src, view(out, self.spot, my_index("dp")), sems[4])

    def away(self, src, out, sems, k):
        _, device = peer_at("dp", 2 * k)
        mine = view(out, self.spot, my_index("dp"))
        return pltpu.make_async_remote_copy(
            src, mine, sems[0].at[k], sems[1].at[k], device_id=device, device_id_type=MESH
        )

    def share(self, src, out, sems, k, first=False):
        count = size_of("dp")
        me = my_index("dp")
        place = view(out, self.spot, lax.rem(me - 2 * k + count, count))
        return pltpu.make_async_remote_copy(
            src if first else place,
            place,
            sems[2].at[k],
            sems[3].at[k],
            device_id={"dp": me + 1 - 2 * lax.rem(me, 2)},
            device_id_type=MESH,
        )

    def start(self, src, out, sems):
        for_each(size_of("dp") // 2 - 1, lambda k: self.away(src, out, sems, k + 1).start())
        self.share(src, out, sems, 0, True).start()
        self.own(src, out, sems).start()

    def step(self, number, src, out, sems):
        if number != 2:
            return

        def pass_on(k):
            self.away(src, out, sems, k + 1).wait_recv()
            self.share(src, out, sems, k + 1).start()

        for_each(size_of("dp") // 2 - 1, pass_on)

    def finish(self, src, out, sems):
        for_each(size_of("dp") // 2 - 1, lambda k: self.away(src, out, sems, k + 1).wait_send())
        self.share(src, out, sems, 0, True).wait()
        for_each(size_of("dp") // 2 - 1, lambda k: self.share(src, out, sems, k + 1).wait())
        self.own(src, out, sems).wait()


class Swap(Task):
    def __init__(self, axis, array, spot=None):
        self.axis, self.array, self.spot = axis, array, spot
        shape = list(array.shape)
        if spot is None:
            shape = shape[1:]
        else:
            shape[spot[0]] = spot[1]
        self.out = jax.ShapeDtypeStruct((size_of(axis) - 1, *shape), array.dtype)
        self.sems = [pltpu.SemaphoreType.DMA((size_of(axis),)) for _ in range(2)]

    def copy(self, src, out, sems, k):
        index, device = peer_at(self.axis, k)
        return pltpu.make_async_remote_copy(
            view(src, self.spot, index),
            out.at[k - 1],
            sems[0].at[k],
            sems[1].at[k],
            device_id=device,
            device_id_type=MESH,
        )

    def start(self, src, out, sems):
        for_each(size_of(self.axis) - 1, lambda k: self.copy(src, out, sems, k + 1).start())

    def finish(self, src, out, sems):
        for_each(size_of(self.axis) - 1, lambda k: self.copy(src, out, sems, k + 1).wait())


class Line(Task):
    axis = "tensor"

    def remote(self, src, dst, sems, way, index):
        target = lax.axis_index("tensor") + (1 - 2 * way)
        return pltpu.make_async_remote_copy(
            src,
            dst,
            sems[0].at[way, index],
            sems[1].at[way, index],
            device_id={"tensor": target},
            device_id_type=MESH,
        )


class LineGather(Line):
    def __init__(self, block):
        self.array = block
        count = size_of("tensor")
        self.out = jax.ShapeDtypeStruct((count, *block.shape), block.dtype)
        self.sems = [
            pltpu.SemaphoreType.DMA((2, count)),
            pltpu.SemaphoreType.DMA((2, count)),
            pltpu.SemaphoreType.DMA,
        ]

    def own(self, src, out, sems):
        return pltpu.make_async_copy(src, out.at[lax.axis_index("tensor")], sems[2])

    def start(self, src, out, sems):
        me, last = lax.axis_index("tensor"), size_of("tensor") - 1
        pl.when(me < last)(lambda: self.remote(src, out.at[me], sems, 0, me).start())
        pl.when(me > 0)(lambda: self.remote(src, out.at[me], sems, 1, me).start())
        self.own(src, out, sems).start()

    def step(self, number, src, out, sems):
        me, last = lax.axis_index("tensor"), size_of("tensor") - 1
        for way, index, here, more in (
            (0, me - number, me >= number, me < last),
            (1, me + number, me + number <= last, me > 0),
        ):

            @pl.when(here)
            def _():
                copy = self.remote(out.at[index], out.at[index], sems, way, index)
                copy.wait_recv()
                pl.when(more)(copy.start)

    def finish(self, src, out, sems):
        me, last = lax.axis_index("tensor"), size_of("tensor") - 1
        for number in range(last + 1):
            for way, index, sent in (
                (0, me - number, (me >= number) & (me < last)),
                (1, me + number, (me + number <= last) & (me > 0)),
            ):
                copy = self.remote(src, out.at[me], sems, way, index)
                pl.when(sent)(copy.wait_send)
        self.own(src, out, sems).wait()


class LineSum(Line):
    place = pltpu.VMEM

    def __init__(self, blocks):
        self.array = blocks
        count = blocks.shape[0]
        self.out = jax.ShapeDtypeStruct((2, *blocks.shape[1:]), blocks.dtype)
        self.sems = [
            pltpu.SemaphoreType.DMA((2, count)),
            pltpu.SemaphoreType.DMA((2, count)),
            pltpu.VMEM((2, *blocks.shape), blocks.dtype),
        ]

    def start(self, src, out, sems):
        self.move(0, src, sems)

    def step(self, number, src, out, sems):
        if number < size_of("tensor") - 1:
            self.move(number, src, sems)

    def routes(self, number):
        me, last = lax.axis_index("tensor"), size_of("tensor") - 1
        up, down = number - me, number - (last - me)
        return (
            (0, last - up, (up >= 0) & (last - up > me), me > 0),
            (1, down, (down >= 0) & (down < me), me < last),
        )

    def move(self, number, src, sems):
        held = sems[2]
        for way, index, sends, follows in self.routes(number):

            @pl.when(sends)
            def _():
                slot = held.at[way, index]

                @pl.when(follows)
                def _():
                    self.remote(slot, slot, sems, way, index).wait_recv()
                    self.add(src, held, way, index)
                    self.remote(slot, slot, sems, way, index).start()

                @pl.when(jnp.logical_not(follows))
                def _():
                    self.remote(src.at[index], slot, sems, way, index).start()

    def add(self, src, held, way, index):
        width = 2 * LANES
        for at in range(0, held.shape[3], width):
            part = held[way, index, :, at : at + width].astype(jnp.float32)
            part += src[index, :, at : at + width].astype(jnp.float32)
            held[way, index, :, at : at + width] = part.astype(held.dtype)

    def finish(self, src, out, sems):
        me, last = lax.axis_index("tensor"), size_of("tensor") - 1
        held = sems[2]
        for way, comes in ((0, me > 0), (1, me < last)):

            @pl.when(comes)
            def _():
                slot = held.at[way, me]
                self.remote(slot, slot, sems, way, me).wait_recv()
                out[way] = held[way, me]

            @pl.when(jnp.logical_not(comes))
            def _():
                out[way] = jnp.zeros(out.shape[1:], out.dtype)

        for number in range(last):
            for way, index, sends, _ in self.routes(number):
                slot = held.at[way, index]
                pl.when(sends)(self.remote(slot, slot, sems, way, index).wait_send)


def exchange(number, *tasks):
    axes = sorted({task.axis for task in tasks})
    if "all" in axes:
        axes = ["all"]
    count = len(tasks)

    def kernel(*refs):
        sources, outs, sems = refs[:count], refs[count : 2 * count], list(refs[2 * count :])
        grouped = []
        for task in tasks:
            grouped.append([sems.pop(0) for _ in task.sems])
        barrier = pltpu.get_barrier_semaphore()

        def greet(axis, k):
            _, device = peer_at(axis, k)
            pl.semaphore_signal(barrier, inc=1, device_id=device, device_id_type=MESH)

        for axis in axes:
            for_each(size_of(axis) - 1, functools.partial(lambda a, k: greet(a, k + 1), axis))
        pl.semaphore_wait(barrier, sum(size_of(axis) - 1 for axis in axes))
        every = list(zip(tasks, sources, outs, grouped))
        for task, src, out, own in every:
            task.start(src, out, own)
        for step in range(1, size_of("tensor")):
            for task, src, out, own in every:
                task.step(step, src, out, own)
        for task, src, out, own in every:
            task.finish(src, out, own)

    return pl.pallas_call(
        kernel,
        out_shape=[task.out for task in tasks],
        in_specs=[pl.BlockSpec(memory_space=task.place) for task in tasks],
        out_specs=[pl.BlockSpec(memory_space=task.place) for task in tasks],
        scratch_shapes=[sem for task in tasks for sem in task.sems],
        compiler_params=pltpu.CompilerParams(
            collective_id=number, has_side_effects=True, vmem_limit_bytes=24 * 2**20
        ),
    )(*[task.array for task in tasks])


def spot_of(block, dim, width):
    grain = LANES if dim == block.ndim - 1 else 16
    return (dim, width) if width % grain == 0 else None


def weight_gather(block, dim):
    return PairGather(block, spot_of(block, dim, block.shape[dim]))


def joined(gathered, block, dim):
    if gathered.ndim == block.ndim:
        return gathered
    moved = jnp.moveaxis(gathered, 0, dim)
    shape = list(block.shape)
    shape[dim] *= gathered.shape[0]
    return moved.reshape(shape)


def grad_swap(term, dim):
    count = size_of("dp")
    width = term.shape[dim] // count
    low = term.astype(jnp.bfloat16)
    spot = spot_of(low, dim, width)
    if spot is None:
        shape = list(low.shape)
        shape[dim : dim + 1] = [count, width]
        low = jnp.moveaxis(low.reshape(shape), dim, 0)
    return Swap("dp", low, spot)


def own_part(term, axis, dim):
    width = term.shape[dim] // size_of(axis)
    return lax.dynamic_slice_in_dim(term, my_index(axis) * width, width, dim)


def summed(own, others):
    return own + jnp.sum(others.astype(jnp.float32), axis=0)


def layer_norm(values, gain, shift):
    centred = values - jnp.mean(values, axis=-1, keepdims=True)
    spread = jnp.mean(centred * centred, axis=-1, keepdims=True)
    return centred * lax.rsqrt(spread + EPSILON) * gain + shift


def exact_gelu(values):
    return jax.nn.gelu(values, approximate=False)


def masked_scores(query, keys, valid_keys, scale):
    scores = jnp.einsum("qhd,khd->hqk", query, keys, preferred_element_type=jnp.float32) * scale
    return jnp.where(valid_keys[None, None, :], scores, NEGATIVE)


def attend(query, keys, values, valid_keys, scale):
    scores = masked_scores(query, keys, valid_keys, scale)
    largest = jnp.max(scores, axis=-1, keepdims=True)
    powers = jnp.exp(scores - largest)
    total = jnp.sum(powers, axis=-1, keepdims=True)
    probs = (powers / total).astype(jnp.bfloat16)
    mixed = jnp.einsum("hqk,khd->qhd", probs, values, preferred_element_type=jnp.float32)
    return (mixed, largest + jnp.log(total))


def attend_back(query, keys, values, valid_keys, scale, log_total, grad_mixed):
    scores = masked_scores(query, keys, valid_keys, scale)
    probs = jnp.exp(scores - log_total)
    grad_probs = jnp.einsum("qhd,khd->hqk", grad_mixed, values, preferred_element_type=jnp.float32)
    inner = jnp.sum(grad_probs * probs, axis=-1, keepdims=True)
    grad_scores = (probs * (grad_probs - inner)).astype(jnp.bfloat16)
    grad_values = jnp.einsum(
        "hqk,qhd->khd", probs.astype(jnp.bfloat16), grad_mixed, preferred_element_type=jnp.float32
    )
    grad_query = (
        jnp.einsum("hqk,khd->qhd", grad_scores, keys, preferred_element_type=jnp.float32) * scale
    )
    grad_keys = (
        jnp.einsum("hqk,qhd->khd", grad_scores, query, preferred_element_type=jnp.float32) * scale
    )
    return (grad_query, grad_keys, grad_values)


def row_validity(counts, seq, rows):
    places = jnp.arange(rows, dtype=jnp.int32)
    owner = places // seq
    position = places - owner * seq
    picks = owner[:, None] == jnp.arange(counts.shape[0], dtype=jnp.int32)[None, :]
    return position < jnp.sum(jnp.where(picks, counts[None, :], 0), axis=1)


def row_sum(part, rows):
    return LineSum(part.astype(jnp.bfloat16).reshape(-1, rows, part.shape[1]))


def row_permutes(part, rows):
    count = size_of("tensor")
    parts = part.reshape(count, rows, part.shape[1])
    others = []
    for k in range(1, count):
        index, _ = peer_at("tensor", k)
        block = lax.dynamic_index_in_dim(parts, index, 0, keepdims=False)
        pairs = [(i, (i + k) % count) for i in range(count)]
        others.append(lax.ppermute(block, "tensor", pairs))
    return others


def on_device(tokens, counts, vectors, fc1_bias, w_qkv, w_out, w_fc1, w_fc2, cotangent):
    tensor_count = lax.axis_size("tensor")
    tensor_index = lax.axis_index("tensor")
    devices = size_of("all")
    model_width = tokens.shape[1]
    vector_size = vectors.size
    small_size = vector_size + fc1_bias.size
    small_rows = -(-small_size // (8 * LANES)) * 8
    small = jnp.concatenate([vectors.reshape(-1), fc1_bias])
    small = jnp.pad(small, (0, small_rows * LANES - small_size)).reshape(small_rows, LANES)
    local_rows = tokens.shape[0]
    block_rows = local_rows * tensor_count
    images = counts.shape[0]
    local_valid = row_validity(counts, block_rows // images, block_rows)
    local_valid = lax.dynamic_slice_in_dim(local_valid, tensor_index * local_rows, local_rows)
    local_valid = local_valid.astype(jnp.float32)[:, None]
    masked_out = local_valid * cotangent
    small_all, gathered_grad, qkv_all, out_all = exchange(
        0,
        Gather("all", small),
        LineGather(masked_out.astype(jnp.bfloat16)),
        weight_gather(w_qkv, 1),
        weight_gather(w_out, 1),
    )
    qkv_all = joined(qkv_all, w_qkv, 1)
    out_all = joined(out_all, w_out, 1)
    gathered_grad = gathered_grad.reshape(block_rows, model_width)
    small_all = small_all.reshape(devices, small_rows * LANES)
    full_vectors = small_all[:, :vector_size].reshape(devices, vectors.shape[0], -1)
    full_vectors = full_vectors.transpose(1, 0, 2).reshape(vectors.shape[0], model_width)
    full_fc1 = small_all[:, vector_size:small_size].reshape(-1)
    normed = layer_norm(tokens, full_vectors[0], full_vectors[1]).astype(jnp.bfloat16)
    (gathered,) = exchange(1, LineGather(normed))
    gathered = gathered.reshape(block_rows, model_width)
    seq = block_rows // images
    width = qkv_all.shape[2]
    hidden_width = w_fc1.shape[1]
    heads_local = width // HEAD_DIM
    scale = HEAD_DIM ** (-0.5)
    block_valid = row_validity(counts, seq, block_rows)
    query_bias = lax.dynamic_slice_in_dim(full_vectors[2], tensor_index * width, width)
    value_bias = lax.dynamic_slice_in_dim(full_vectors[3], tensor_index * width, width)
    hidden_bias = lax.dynamic_slice_in_dim(full_fc1, tensor_index * hidden_width, hidden_width)
    projected = jnp.einsum("rd,kde->kre", gathered, qkv_all, preferred_element_type=jnp.float32)
    query = (
        (projected[0] + query_bias).astype(jnp.bfloat16).reshape(block_rows, heads_local, HEAD_DIM)
    )
    keys = projected[1].astype(jnp.bfloat16).reshape(block_rows, heads_local, HEAD_DIM)
    values = (
        (projected[2] + value_bias).astype(jnp.bfloat16).reshape(block_rows, heads_local, HEAD_DIM)
    )
    mixed_one, total_one = attend(query, keys, values, block_valid, scale)
    mixed_all = mixed_one.reshape(block_rows, width).astype(jnp.bfloat16)
    attn_part = jnp.dot(mixed_all, out_all, preferred_element_type=jnp.float32)
    attn_others, fc1_all = exchange(2, row_sum(attn_part, local_rows), weight_gather(w_fc1, 0))
    fc1_all = joined(fc1_all, w_fc1, 0)
    attn_local = summed(own_part(attn_part, "tensor", 0), attn_others)
    middle = tokens + local_valid * (attn_local + full_vectors[4])
    normed2 = layer_norm(middle, full_vectors[5], full_vectors[6]).astype(jnp.bfloat16)
    gathered2, fc2_all = exchange(3, LineGather(normed2), weight_gather(w_fc2, 1))
    fc2_all = joined(fc2_all, w_fc2, 1)
    gathered2 = gathered2.reshape(block_rows, model_width)
    pre = jnp.dot(gathered2, fc1_all, preferred_element_type=jnp.float32) + hidden_bias
    hidden_float, gelu_back = jax.vjp(exact_gelu, pre)
    hidden = hidden_float.astype(jnp.bfloat16)
    mlp_part = jnp.dot(hidden, fc2_all, preferred_element_type=jnp.float32)
    grad_shift2 = jnp.sum(masked_out, axis=0)
    fc2_term = jnp.einsum("rf,rd->fd", hidden, gathered_grad, preferred_element_type=jnp.float32)
    grad_hidden = jnp.einsum(
        "rd,fd->rf", gathered_grad, fc2_all, preferred_element_type=jnp.float32
    )
    grad_pre = gelu_back(grad_hidden)[0].astype(jnp.bfloat16)
    hidden_bias_grad = jnp.sum(grad_pre.astype(jnp.float32), axis=0)
    fc1_term = jnp.einsum("rd,rf->df", gathered2, grad_pre, preferred_element_type=jnp.float32)
    normed2_part = jnp.einsum("rf,df->rd", grad_pre, fc1_all, preferred_element_type=jnp.float32)
    normed2_others, fc2_others = exchange(
        4, row_sum(normed2_part, local_rows), grad_swap(fc2_term, 1)
    )
    grad_normed2 = summed(own_part(normed2_part, "tensor", 0), normed2_others)
    fc2_grad = summed(own_part(fc2_term, "dp", 1), fc2_others)
    second_norm, second_back = jax.vjp(layer_norm, middle, full_vectors[5], full_vectors[6])
    grad_through, gain2_grad, shift2_grad = second_back(grad_normed2)
    grad_middle = cotangent + grad_through
    masked_middle = local_valid * grad_middle
    out_bias_grad = jnp.sum(masked_middle, axis=0)
    gathered_attn, fc1_others = exchange(
        5, LineGather(masked_middle.astype(jnp.bfloat16)), grad_swap(fc1_term, 0)
    )
    fc1_grad = summed(own_part(fc1_term, "dp", 0), fc1_others)
    gathered_attn, mlp_low = lax.optimization_barrier(
        (gathered_attn, mlp_part.astype(jnp.bfloat16))
    )
    mlp_others = row_permutes(mlp_low, local_rows)
    mlp_local = own_part(mlp_part, "tensor", 0)
    for block in mlp_others:
        mlp_local = mlp_local + block.astype(jnp.float32)
    layer_out = middle + local_valid * (mlp_local + full_vectors[7])
    gathered_attn = gathered_attn.reshape(block_rows, model_width)
    out_term = jnp.einsum("re,rd->ed", mixed_all, gathered_attn, preferred_element_type=jnp.float32)
    grad_mixed = jnp.einsum("rd,ed->re", gathered_attn, out_all, preferred_element_type=jnp.float32)
    grad_mixed = grad_mixed.astype(jnp.bfloat16).reshape(block_rows, heads_local, HEAD_DIM)
    grad_q, grad_k, grad_v = attend_back(
        query, keys, values, block_valid, scale, total_one, grad_mixed
    )
    grad_query = grad_q.reshape(block_rows, width).astype(jnp.bfloat16)
    grad_keys = grad_k.reshape(block_rows, width).astype(jnp.bfloat16)
    grad_values = grad_v.reshape(block_rows, width).astype(jnp.bfloat16)
    stacked = jnp.stack([grad_query, grad_keys, grad_values])
    query_bias_grad = jnp.sum(grad_query.astype(jnp.float32), axis=0)
    value_bias_grad = jnp.sum(grad_values.astype(jnp.float32), axis=0)
    qkv_term = jnp.einsum("rd,kre->kde", gathered, stacked, preferred_element_type=jnp.float32)
    normed_part = jnp.einsum("kre,kde->rd", stacked, qkv_all, preferred_element_type=jnp.float32)
    normed_others, qkv_others, out_others = exchange(
        6, row_sum(normed_part, local_rows), grad_swap(qkv_term, 1), grad_swap(out_term, 1)
    )
    grad_normed = summed(own_part(normed_part, "tensor", 0), normed_others)
    qkv_grad = summed(own_part(qkv_term, "dp", 1), qkv_others)
    out_grad = summed(own_part(out_term, "dp", 1), out_others)
    first_norm, first_back = jax.vjp(layer_norm, tokens, full_vectors[0], full_vectors[1])
    grad_input_norm, gain1_grad, shift1_grad = first_back(grad_normed)
    input_grad = grad_middle + grad_input_norm
    zeros_model = jnp.zeros((model_width,), jnp.float32)
    query_bias_full = lax.dynamic_update_slice_in_dim(
        zeros_model, query_bias_grad, tensor_index * width, 0
    )
    value_bias_full = lax.dynamic_update_slice_in_dim(
        zeros_model, value_bias_grad, tensor_index * width, 0
    )
    vector_terms = jnp.stack(
        [
            gain1_grad,
            shift1_grad,
            query_bias_full,
            value_bias_full,
            out_bias_grad,
            gain2_grad,
            shift2_grad,
            grad_shift2,
        ]
    )
    zeros_hidden = jnp.zeros((full_fc1.shape[0],), jnp.float32)
    hidden_bias_full = lax.dynamic_update_slice_in_dim(
        zeros_hidden, hidden_bias_grad, tensor_index * hidden_width, 0
    )
    vector_blocks = vector_terms.reshape(vectors.shape[0], devices, -1).transpose(1, 0, 2)
    small_terms = jnp.concatenate(
        [vector_blocks.reshape(devices, -1), hidden_bias_full.reshape(devices, -1)], axis=1
    )
    small_terms = jnp.pad(small_terms, ((0, 0), (0, small_rows * LANES - small_size)))
    small_terms = small_terms.reshape(devices, small_rows, LANES)
    (small_others,) = exchange(7, Swap("all", small_terms))
    small_grad = summed(own_part(small_terms, "all", 0)[0], small_others).reshape(-1)
    vectors_grad = small_grad[:vector_size].reshape(vectors.shape)
    fc1_bias_grad = small_grad[vector_size:small_size]
    return (
        layer_out,
        input_grad,
        vectors_grad,
        fc1_bias_grad,
        qkv_grad,
        out_grad,
        fc1_grad,
        fc2_grad,
    )


def solution(mesh):
    placed = (
        P(("dp", "tensor"), None),
        P("dp"),
        P(None, ("dp", "tensor")),
        P(("dp", "tensor")),
        P(None, "dp", "tensor"),
        P("tensor", "dp"),
        P("dp", "tensor"),
        P("tensor", "dp"),
        P(("dp", "tensor"), None),
    )
    return jax.shard_map(
        on_device,
        mesh=mesh,
        in_specs=placed,
        out_specs=(
            P(("dp", "tensor"), None),
            P(("dp", "tensor"), None),
            P(None, ("dp", "tensor")),
            P(("dp", "tensor")),
            P(None, "dp", "tensor"),
            P("tensor", "dp"),
            P("dp", "tensor"),
            P("tensor", "dp"),
        ),
        check_vma=False,
    )
```

```python
import functools

import jax
import jax.numpy as jnp
from jax import lax
from jax.experimental import pallas as pl
from jax.experimental.pallas import tpu as pltpu
from jax.sharding import PartitionSpec as P

HEAD_DIM = 64


EPSILON = 1e-06
NEGATIVE = -1e30
MESH = pl.DeviceIdType.MESH
LANES = 128


def peer_at(axis, k):
    if axis == "all":
        dp, tensor = lax.axis_size("dp"), lax.axis_size("tensor")
        index = lax.rem(lax.axis_index("dp") * tensor + lax.axis_index("tensor") + k, dp * tensor)
        return index, {"dp": index // tensor, "tensor": lax.rem(index, tensor)}
    index = lax.rem(lax.axis_index(axis) + k, lax.axis_size(axis))
    return index, {axis: index}


def my_index(axis):
    if axis == "all":
        return lax.axis_index("dp") * lax.axis_size("tensor") + lax.axis_index("tensor")
    return lax.axis_index(axis)


def size_of(axis):
    if axis == "all":
        return lax.axis_size("dp") * lax.axis_size("tensor")
    return lax.axis_size(axis)


def view(ref, spot, index):
    if spot is None:
        return ref.at[index]
    dim, width = spot
    place = pl.ds(pl.multiple_of(index * width, width), width)
    return ref.at[tuple([slice(None)] * dim + [place])]


def for_each(count, body):
    lax.fori_loop(0, count, lambda k, carry: (body(k), carry)[1], 0)


class Task:
    place = pl.ANY

    def step(self, number, src, out, sems):
        pass


class Gather(Task):
    def __init__(self, axis, block, spot=None):
        self.axis, self.array, self.spot = axis, block, spot
        shape = list(block.shape)
        if spot is None:
            shape = [size_of(axis)] + shape
        else:
            shape[spot[0]] *= size_of(axis)
        self.out = jax.ShapeDtypeStruct(tuple(shape), block.dtype)
        self.sems = [
            pltpu.SemaphoreType.DMA((size_of(axis),)),
            pltpu.SemaphoreType.DMA((size_of(axis),)),
            pltpu.SemaphoreType.DMA,
        ]

    def own(self, src, out, sems):
        return pltpu.make_async_copy(src, view(out, self.spot, my_index(self.axis)), sems[2])

    def copy(self, src, out, sems, k):
        _, device = peer_at(self.axis, k)
        mine = view(out, self.spot, my_index(self.axis))
        return pltpu.make_async_remote_copy(
            src, mine, sems[0].at[k], sems[1].at[k], device_id=device, device_id_type=MESH
        )

    def start(self, src, out, sems):
        for_each(size_of(self.axis) - 1, lambda k: self.copy(src, out, sems, k + 1).start())
        self.own(src, out, sems).start()

    def finish(self, src, out, sems):
        for_each(size_of(self.axis) - 1, lambda k: self.copy(src, out, sems, k + 1).wait())
        self.own(src, out, sems).wait()


class PairGather(Gather):
    def __init__(self, block, spot=None):
        super().__init__("dp", block, spot)
        half = size_of("dp") // 2
        self.sems = [pltpu.SemaphoreType.DMA((half,)) for _ in range(4)]
        self.sems.append(pltpu.SemaphoreType.DMA)

    def own(self, src, out, sems):
        return pltpu.make_async_copy(src, view(out, self.spot, my_index("dp")), sems[4])

    def away(self, src, out, sems, k):
        _, device = peer_at("dp", 2 * k)
        mine = view(out, self.spot, my_index("dp"))
        return pltpu.make_async_remote_copy(
            src, mine, sems[0].at[k], sems[1].at[k], device_id=device, device_id_type=MESH
        )

    def share(self, src, out, sems, k, first=False):
        count = size_of("dp")
        me = my_index("dp")
        place = view(out, self.spot, lax.rem(me - 2 * k + count, count))
        return pltpu.make_async_remote_copy(
            src if first else place,
            place,
            sems[2].at[k],
            sems[3].at[k],
            device_id={"dp": me + 1 - 2 * lax.rem(me, 2)},
            device_id_type=MESH,
        )

    def start(self, src, out, sems):
        for_each(size_of("dp") // 2 - 1, lambda k: self.away(src, out, sems, k + 1).start())
        self.share(src, out, sems, 0, True).start()
        self.own(src, out, sems).start()

    def step(self, number, src, out, sems):
        if number != size_of("tensor") - 1:
            return

        def pass_on(k):
            self.away(src, out, sems, k + 1).wait_recv()
            self.share(src, out, sems, k + 1).start()

        for_each(size_of("dp") // 2 - 1, pass_on)

    def finish(self, src, out, sems):
        for_each(size_of("dp") // 2 - 1, lambda k: self.away(src, out, sems, k + 1).wait_send())
        self.share(src, out, sems, 0, True).wait()
        for_each(size_of("dp") // 2 - 1, lambda k: self.share(src, out, sems, k + 1).wait())
        self.own(src, out, sems).wait()


class Swap(Task):
    def __init__(self, axis, array, spot=None):
        self.axis, self.array, self.spot = axis, array, spot
        shape = list(array.shape)
        if spot is None:
            shape = shape[1:]
        else:
            shape[spot[0]] = spot[1]
        self.out = jax.ShapeDtypeStruct((size_of(axis) - 1, *shape), array.dtype)
        self.sems = [pltpu.SemaphoreType.DMA((size_of(axis),)) for _ in range(2)]

    def copy(self, src, out, sems, k):
        index, device = peer_at(self.axis, k)
        return pltpu.make_async_remote_copy(
            view(src, self.spot, index),
            out.at[k - 1],
            sems[0].at[k],
            sems[1].at[k],
            device_id=device,
            device_id_type=MESH,
        )

    def start(self, src, out, sems):
        for_each(size_of(self.axis) - 1, lambda k: self.copy(src, out, sems, k + 1).start())

    def finish(self, src, out, sems):
        for_each(size_of(self.axis) - 1, lambda k: self.copy(src, out, sems, k + 1).wait())


class PairSwap(Task):
    axis = "dp"
    place = pltpu.VMEM

    def __init__(self, array, spot=None):
        self.array, self.spot = array, spot
        shape = list(array.shape)
        if spot is None:
            shape = shape[1:]
        else:
            shape[spot[0]] = spot[1]
        half = size_of("dp") // 2
        self.out = jax.ShapeDtypeStruct((half, *shape), array.dtype)
        self.sems = [pltpu.SemaphoreType.DMA((half,)) for _ in range(4)]
        self.sems.append(pltpu.VMEM((half, *shape), array.dtype))

    def share(self, src, dst, sems, k):
        me = my_index("dp")
        partner = me + 1 - 2 * lax.rem(me, 2)
        return pltpu.make_async_remote_copy(
            view(src, self.spot, lax.rem(partner + 2 * k, size_of("dp"))),
            dst.at[k],
            sems[0].at[k],
            sems[1].at[k],
            device_id={"dp": partner},
            device_id_type=MESH,
        )

    def away(self, out, sems, k):
        _, device = peer_at("dp", 2 * k)
        return pltpu.make_async_remote_copy(
            sems[4].at[k],
            out.at[k],
            sems[2].at[k],
            sems[3].at[k],
            device_id=device,
            device_id_type=MESH,
        )

    def start(self, src, out, sems):
        others = size_of("dp") // 2 - 1
        for_each(others, lambda k: self.share(src, sems[4], sems, k + 1).start())
        self.share(src, out, sems, 0).start()

    def step(self, number, src, out, sems):
        if number != 1:
            return

        def pass_on(k):
            self.share(src, sems[4], sems, k).wait_recv()
            index, _ = peer_at("dp", 2 * k)
            own = view(src, self.spot, index)[...].astype(jnp.float32)
            sems[4][k] = (sems[4][k].astype(jnp.float32) + own).astype(src.dtype)
            self.away(out, sems, k).start()

        for_each(size_of("dp") // 2 - 1, lambda k: pass_on(k + 1))

    def finish(self, src, out, sems):
        others = size_of("dp") // 2 - 1
        for_each(others, lambda k: self.share(src, sems[4], sems, k + 1).wait_send())
        self.share(src, out, sems, 0).wait()
        for_each(others, lambda k: self.away(out, sems, k + 1).wait())


class Line(Task):
    axis = "tensor"

    def remote(self, src, dst, sems, way, index):
        target = lax.axis_index("tensor") + (1 - 2 * way)
        return pltpu.make_async_remote_copy(
            src,
            dst,
            sems[0].at[way, index],
            sems[1].at[way, index],
            device_id={"tensor": target},
            device_id_type=MESH,
        )


class LineGather(Line):
    def __init__(self, block):
        self.array = block
        count = size_of("tensor")
        self.out = jax.ShapeDtypeStruct((count, *block.shape), block.dtype)
        self.sems = [
            pltpu.SemaphoreType.DMA((2, count)),
            pltpu.SemaphoreType.DMA((2, count)),
            pltpu.SemaphoreType.DMA,
        ]

    def own(self, src, out, sems):
        return pltpu.make_async_copy(src, out.at[lax.axis_index("tensor")], sems[2])

    def start(self, src, out, sems):
        me, last = lax.axis_index("tensor"), size_of("tensor") - 1
        pl.when(me < last)(lambda: self.remote(src, out.at[me], sems, 0, me).start())
        pl.when(me > 0)(lambda: self.remote(src, out.at[me], sems, 1, me).start())
        self.own(src, out, sems).start()

    def step(self, number, src, out, sems):
        me, last = lax.axis_index("tensor"), size_of("tensor") - 1
        for way, index, here, more in (
            (0, me - number, me >= number, me < last),
            (1, me + number, me + number <= last, me > 0),
        ):

            @pl.when(here)
            def _():
                copy = self.remote(out.at[index], out.at[index], sems, way, index)
                copy.wait_recv()
                pl.when(more)(copy.start)

    def finish(self, src, out, sems):
        me, last = lax.axis_index("tensor"), size_of("tensor") - 1
        for number in range(last + 1):
            for way, index, sent in (
                (0, me - number, (me >= number) & (me < last)),
                (1, me + number, (me + number <= last) & (me > 0)),
            ):
                copy = self.remote(src, out.at[me], sems, way, index)
                pl.when(sent)(copy.wait_send)
        self.own(src, out, sems).wait()


class LineSum(Line):
    place = pltpu.VMEM

    def __init__(self, blocks):
        self.array = blocks
        count = blocks.shape[0]
        self.out = jax.ShapeDtypeStruct((2, *blocks.shape[1:]), blocks.dtype)
        self.sems = [
            pltpu.SemaphoreType.DMA((2, count)),
            pltpu.SemaphoreType.DMA((2, count)),
            pltpu.VMEM((2, *blocks.shape), blocks.dtype),
        ]

    def start(self, src, out, sems):
        self.move(0, src, sems)

    def step(self, number, src, out, sems):
        if number < size_of("tensor") - 1:
            self.move(number, src, sems)

    def routes(self, number):
        me, last = lax.axis_index("tensor"), size_of("tensor") - 1
        up, down = number - me, number - (last - me)
        return (
            (0, last - up, (up >= 0) & (last - up > me), me > 0),
            (1, down, (down >= 0) & (down < me), me < last),
        )

    def move(self, number, src, sems):
        held = sems[2]
        for way, index, sends, follows in self.routes(number):

            @pl.when(sends)
            def _():
                slot = held.at[way, index]

                @pl.when(follows)
                def _():
                    self.remote(slot, slot, sems, way, index).wait_recv()
                    self.add(src, held, way, index)
                    self.remote(slot, slot, sems, way, index).start()

                @pl.when(jnp.logical_not(follows))
                def _():
                    self.remote(src.at[index], slot, sems, way, index).start()

    def add(self, src, held, way, index):
        width = 2 * LANES
        for at in range(0, held.shape[3], width):
            part = held[way, index, :, at : at + width].astype(jnp.float32)
            part += src[index, :, at : at + width].astype(jnp.float32)
            held[way, index, :, at : at + width] = part.astype(held.dtype)

    def finish(self, src, out, sems):
        me, last = lax.axis_index("tensor"), size_of("tensor") - 1
        held = sems[2]
        for way, comes in ((0, me > 0), (1, me < last)):

            @pl.when(comes)
            def _():
                slot = held.at[way, me]
                self.remote(slot, slot, sems, way, me).wait_recv()
                out[way] = held[way, me]

            @pl.when(jnp.logical_not(comes))
            def _():
                out[way] = jnp.zeros(out.shape[1:], out.dtype)

        for number in range(last):
            for way, index, sends, _ in self.routes(number):
                slot = held.at[way, index]
                pl.when(sends)(self.remote(slot, slot, sems, way, index).wait_send)


def exchange(number, *tasks):
    axes = sorted({task.axis for task in tasks})
    if "all" in axes:
        axes = ["all"]
    count = len(tasks)

    def kernel(*refs):
        sources, outs, sems = refs[:count], refs[count : 2 * count], list(refs[2 * count :])
        grouped = []
        for task in tasks:
            grouped.append([sems.pop(0) for _ in task.sems])
        barrier = pltpu.get_barrier_semaphore()

        def greet(axis, k):
            _, device = peer_at(axis, k)
            pl.semaphore_signal(barrier, inc=1, device_id=device, device_id_type=MESH)

        for axis in axes:
            for_each(size_of(axis) - 1, functools.partial(lambda a, k: greet(a, k + 1), axis))
        pl.semaphore_wait(barrier, sum(size_of(axis) - 1 for axis in axes))
        every = list(zip(tasks, sources, outs, grouped))
        for task, src, out, own in every:
            task.start(src, out, own)
        by_wait = sorted(every, key=lambda entry: isinstance(entry[0], Line))
        for step in range(1, size_of("tensor")):
            for task, src, out, own in by_wait:
                task.step(step, src, out, own)
        for task, src, out, own in every:
            task.finish(src, out, own)

    return pl.pallas_call(
        kernel,
        out_shape=[task.out for task in tasks],
        in_specs=[pl.BlockSpec(memory_space=task.place) for task in tasks],
        out_specs=[pl.BlockSpec(memory_space=task.place) for task in tasks],
        scratch_shapes=[sem for task in tasks for sem in task.sems],
        compiler_params=pltpu.CompilerParams(
            collective_id=number, has_side_effects=True, vmem_limit_bytes=40 * 2**20
        ),
    )(*[task.array for task in tasks])


def spot_of(block, dim, width):
    grain = LANES if dim == block.ndim - 1 else 16
    return (dim, width) if width % grain == 0 else None


def weight_gather(block, dim):
    return PairGather(block, spot_of(block, dim, block.shape[dim]))


def joined(gathered, block, dim):
    if gathered.ndim == block.ndim:
        return gathered
    moved = jnp.moveaxis(gathered, 0, dim)
    shape = list(block.shape)
    shape[dim] *= gathered.shape[0]
    return moved.reshape(shape)


def grad_swap(term, dim):
    count = size_of("dp")
    width = term.shape[dim] // count
    low = term.astype(jnp.bfloat16)
    spot = spot_of(low, dim, width)
    if spot is None:
        shape = list(low.shape)
        shape[dim : dim + 1] = [count, width]
        low = jnp.moveaxis(low.reshape(shape), dim, 0)
    return PairSwap(low, spot)


def own_part(term, axis, dim):
    width = term.shape[dim] // size_of(axis)
    return lax.dynamic_slice_in_dim(term, my_index(axis) * width, width, dim)


def summed(own, others):
    return own + jnp.sum(others.astype(jnp.float32), axis=0)


def normalized(values):
    centred = values - jnp.mean(values, axis=-1, keepdims=True)
    spread = jnp.mean(centred * centred, axis=-1, keepdims=True)
    return centred * lax.rsqrt(spread + EPSILON)


def layer_norm(values, gain, shift):
    return normalized(values) * gain + shift


def exact_gelu(values):
    return jax.nn.gelu(values, approximate=False)


def masked_scores(query, keys, valid_keys, scale):
    scores = jnp.einsum("qhd,khd->hqk", query, keys, preferred_element_type=jnp.float32) * scale
    return jnp.where(valid_keys[None, None, :], scores, NEGATIVE)


def attend(query, keys, values, valid_keys, scale):
    scores = masked_scores(query, keys, valid_keys, scale)
    largest = jnp.max(scores, axis=-1, keepdims=True)
    powers = jnp.exp(scores - largest)
    total = jnp.sum(powers, axis=-1, keepdims=True)
    probs = (powers / total).astype(jnp.bfloat16)
    mixed = jnp.einsum("hqk,khd->qhd", probs, values, preferred_element_type=jnp.float32)
    return (mixed, largest + jnp.log(total))


def attend_back(query, keys, values, valid_keys, scale, log_total, grad_mixed):
    scores = masked_scores(query, keys, valid_keys, scale)
    probs = jnp.exp(scores - log_total)
    grad_probs = jnp.einsum("qhd,khd->hqk", grad_mixed, values, preferred_element_type=jnp.float32)
    inner = jnp.sum(grad_probs * probs, axis=-1, keepdims=True)
    grad_scores = (probs * (grad_probs - inner)).astype(jnp.bfloat16)
    grad_values = jnp.einsum(
        "hqk,qhd->khd", probs.astype(jnp.bfloat16), grad_mixed, preferred_element_type=jnp.float32
    )
    grad_query = (
        jnp.einsum("hqk,khd->qhd", grad_scores, keys, preferred_element_type=jnp.float32) * scale
    )
    grad_keys = (
        jnp.einsum("hqk,qhd->khd", grad_scores, query, preferred_element_type=jnp.float32) * scale
    )
    return (grad_query, grad_keys, grad_values)


def row_validity(counts, seq, rows):
    places = jnp.arange(rows, dtype=jnp.int32)
    owner = places // seq
    position = places - owner * seq
    picks = owner[:, None] == jnp.arange(counts.shape[0], dtype=jnp.int32)[None, :]
    return position < jnp.sum(jnp.where(picks, counts[None, :], 0), axis=1)


def row_sum(part, rows):
    return LineSum(part.astype(jnp.bfloat16).reshape(-1, rows, part.shape[1]))


def row_permutes(part, rows):
    count = size_of("tensor")
    parts = part.reshape(count, rows, part.shape[1])
    others = []
    for k in range(1, count):
        index, _ = peer_at("tensor", k)
        block = lax.dynamic_index_in_dim(parts, index, 0, keepdims=False)
        pairs = [(i, (i + k) % count) for i in range(count)]
        others.append(lax.ppermute(block, "tensor", pairs))
    return others


def on_device(tokens, counts, vectors, fc1_bias, w_qkv, w_out, w_fc1, w_fc2, cotangent):
    tensor_count = lax.axis_size("tensor")
    tensor_index = lax.axis_index("tensor")
    devices = size_of("all")
    model_width = tokens.shape[1]
    vector_size = vectors.size
    small_size = vector_size + fc1_bias.size
    small_rows = -(-small_size // (8 * LANES)) * 8
    small = jnp.concatenate([vectors.reshape(-1), fc1_bias])
    small = jnp.pad(small, (0, small_rows * LANES - small_size)).reshape(small_rows, LANES)
    local_rows = tokens.shape[0]
    block_rows = local_rows * tensor_count
    images = counts.shape[0]
    local_valid = row_validity(counts, block_rows // images, block_rows)
    local_valid = lax.dynamic_slice_in_dim(local_valid, tensor_index * local_rows, local_rows)
    local_valid = local_valid.astype(jnp.float32)[:, None]
    masked_out = local_valid * cotangent
    small_all, unscaled, gathered_grad, qkv_all, out_all, fc1_all, fc2_all = exchange(
        0,
        Gather("all", small),
        LineGather(normalized(tokens).astype(jnp.bfloat16)),
        LineGather(masked_out.astype(jnp.bfloat16)),
        weight_gather(w_qkv, 1),
        weight_gather(w_out, 1),
        weight_gather(w_fc1, 0),
        weight_gather(w_fc2, 1),
    )
    qkv_all = joined(qkv_all, w_qkv, 1)
    out_all = joined(out_all, w_out, 1)
    fc1_all = joined(fc1_all, w_fc1, 0)
    fc2_all = joined(fc2_all, w_fc2, 1)
    gathered_grad = gathered_grad.reshape(block_rows, model_width)
    small_all = small_all.reshape(devices, small_rows * LANES)
    full_vectors = small_all[:, :vector_size].reshape(devices, vectors.shape[0], -1)
    full_vectors = full_vectors.transpose(1, 0, 2).reshape(vectors.shape[0], model_width)
    full_fc1 = small_all[:, vector_size:small_size].reshape(-1)
    unscaled = unscaled.reshape(block_rows, model_width).astype(jnp.float32)
    gathered = (unscaled * full_vectors[0] + full_vectors[1]).astype(jnp.bfloat16)
    seq = block_rows // images
    width = qkv_all.shape[2]
    hidden_width = w_fc1.shape[1]
    heads_local = width // HEAD_DIM
    scale = HEAD_DIM ** (-0.5)
    block_valid = row_validity(counts, seq, block_rows)
    query_bias = lax.dynamic_slice_in_dim(full_vectors[2], tensor_index * width, width)
    value_bias = lax.dynamic_slice_in_dim(full_vectors[3], tensor_index * width, width)
    hidden_bias = lax.dynamic_slice_in_dim(full_fc1, tensor_index * hidden_width, hidden_width)
    projected = jnp.einsum("rd,kde->kre", gathered, qkv_all, preferred_element_type=jnp.float32)
    query = (
        (projected[0] + query_bias).astype(jnp.bfloat16).reshape(block_rows, heads_local, HEAD_DIM)
    )
    keys = projected[1].astype(jnp.bfloat16).reshape(block_rows, heads_local, HEAD_DIM)
    values = (
        (projected[2] + value_bias).astype(jnp.bfloat16).reshape(block_rows, heads_local, HEAD_DIM)
    )
    mixed_one, total_one = attend(query, keys, values, block_valid, scale)
    mixed_all = mixed_one.reshape(block_rows, width).astype(jnp.bfloat16)
    attn_part = jnp.dot(mixed_all, out_all, preferred_element_type=jnp.float32)
    (attn_others,) = exchange(1, row_sum(attn_part, local_rows))
    attn_local = summed(own_part(attn_part, "tensor", 0), attn_others)
    middle = tokens + local_valid * (attn_local + full_vectors[4])
    normed2 = layer_norm(middle, full_vectors[5], full_vectors[6]).astype(jnp.bfloat16)
    (gathered2,) = exchange(2, LineGather(normed2))
    gathered2 = gathered2.reshape(block_rows, model_width)
    pre = jnp.dot(gathered2, fc1_all, preferred_element_type=jnp.float32) + hidden_bias
    hidden_float, gelu_back = jax.vjp(exact_gelu, pre)
    hidden = hidden_float.astype(jnp.bfloat16)
    mlp_part = jnp.dot(hidden, fc2_all, preferred_element_type=jnp.float32)
    grad_shift2 = jnp.sum(masked_out, axis=0)
    fc2_term = jnp.einsum("rf,rd->fd", hidden, gathered_grad, preferred_element_type=jnp.float32)
    grad_hidden = jnp.einsum(
        "rd,fd->rf", gathered_grad, fc2_all, preferred_element_type=jnp.float32
    )
    grad_pre = gelu_back(grad_hidden)[0].astype(jnp.bfloat16)
    hidden_bias_grad = jnp.sum(grad_pre.astype(jnp.float32), axis=0)
    fc1_term = jnp.einsum("rd,rf->df", gathered2, grad_pre, preferred_element_type=jnp.float32)
    normed2_part = jnp.einsum("rf,df->rd", grad_pre, fc1_all, preferred_element_type=jnp.float32)
    normed2_others, fc2_others = exchange(
        3, row_sum(normed2_part, local_rows), grad_swap(fc2_term, 1)
    )
    grad_normed2 = summed(own_part(normed2_part, "tensor", 0), normed2_others)
    fc2_grad = summed(own_part(fc2_term, "dp", 1), fc2_others)
    second_norm, second_back = jax.vjp(layer_norm, middle, full_vectors[5], full_vectors[6])
    grad_through, gain2_grad, shift2_grad = second_back(grad_normed2)
    grad_middle = cotangent + grad_through
    masked_middle = local_valid * grad_middle
    out_bias_grad = jnp.sum(masked_middle, axis=0)
    gathered_attn, fc1_others = exchange(
        4, LineGather(masked_middle.astype(jnp.bfloat16)), grad_swap(fc1_term, 0)
    )
    fc1_grad = summed(own_part(fc1_term, "dp", 0), fc1_others)
    gathered_attn, mlp_low = lax.optimization_barrier(
        (gathered_attn, mlp_part.astype(jnp.bfloat16))
    )
    mlp_others = row_permutes(mlp_low, local_rows)
    mlp_local = own_part(mlp_part, "tensor", 0)
    for block in mlp_others:
        mlp_local = mlp_local + block.astype(jnp.float32)
    layer_out = middle + local_valid * (mlp_local + full_vectors[7])
    gathered_attn = gathered_attn.reshape(block_rows, model_width)
    out_term = jnp.einsum("re,rd->ed", mixed_all, gathered_attn, preferred_element_type=jnp.float32)
    grad_mixed = jnp.einsum("rd,ed->re", gathered_attn, out_all, preferred_element_type=jnp.float32)
    grad_mixed = grad_mixed.astype(jnp.bfloat16).reshape(block_rows, heads_local, HEAD_DIM)
    grad_q, grad_k, grad_v = attend_back(
        query, keys, values, block_valid, scale, total_one, grad_mixed
    )
    grad_query = grad_q.reshape(block_rows, width).astype(jnp.bfloat16)
    grad_keys = grad_k.reshape(block_rows, width).astype(jnp.bfloat16)
    grad_values = grad_v.reshape(block_rows, width).astype(jnp.bfloat16)
    stacked = jnp.stack([grad_query, grad_keys, grad_values])
    query_bias_grad = jnp.sum(grad_query.astype(jnp.float32), axis=0)
    value_bias_grad = jnp.sum(grad_values.astype(jnp.float32), axis=0)
    qkv_term = jnp.einsum("rd,kre->kde", gathered, stacked, preferred_element_type=jnp.float32)
    normed_part = jnp.einsum("kre,kde->rd", stacked, qkv_all, preferred_element_type=jnp.float32)
    gain1_grad = jnp.sum(normed_part * unscaled, axis=0)
    shift1_grad = jnp.sum(normed_part, axis=0)
    zeros_model = jnp.zeros((model_width,), jnp.float32)
    query_bias_full = lax.dynamic_update_slice_in_dim(
        zeros_model, query_bias_grad, tensor_index * width, 0
    )
    value_bias_full = lax.dynamic_update_slice_in_dim(
        zeros_model, value_bias_grad, tensor_index * width, 0
    )
    vector_terms = jnp.stack(
        [
            gain1_grad,
            shift1_grad,
            query_bias_full,
            value_bias_full,
            out_bias_grad,
            gain2_grad,
            shift2_grad,
            grad_shift2,
        ]
    )
    zeros_hidden = jnp.zeros((full_fc1.shape[0],), jnp.float32)
    hidden_bias_full = lax.dynamic_update_slice_in_dim(
        zeros_hidden, hidden_bias_grad, tensor_index * hidden_width, 0
    )
    vector_blocks = vector_terms.reshape(vectors.shape[0], devices, -1).transpose(1, 0, 2)
    small_terms = jnp.concatenate(
        [vector_blocks.reshape(devices, -1), hidden_bias_full.reshape(devices, -1)], axis=1
    )
    small_terms = jnp.pad(small_terms, ((0, 0), (0, small_rows * LANES - small_size)))
    small_terms = small_terms.reshape(devices, small_rows, LANES)
    normed_others, qkv_others, out_others, small_others = exchange(
        5,
        row_sum(normed_part, local_rows),
        grad_swap(qkv_term, 1),
        grad_swap(out_term, 1),
        Swap("all", small_terms),
    )
    grad_normed = summed(own_part(normed_part, "tensor", 0), normed_others)
    qkv_grad = summed(own_part(qkv_term, "dp", 1), qkv_others)
    out_grad = summed(own_part(out_term, "dp", 1), out_others)
    first_norm, first_back = jax.vjp(layer_norm, tokens, full_vectors[0], full_vectors[1])
    grad_input_norm, _, _ = first_back(grad_normed)
    input_grad = grad_middle + grad_input_norm
    small_grad = summed(own_part(small_terms, "all", 0)[0], small_others).reshape(-1)
    vectors_grad = small_grad[:vector_size].reshape(vectors.shape)
    fc1_bias_grad = small_grad[vector_size:small_size]
    return (
        layer_out,
        input_grad,
        vectors_grad,
        fc1_bias_grad,
        qkv_grad,
        out_grad,
        fc1_grad,
        fc2_grad,
    )


def solution(mesh):
    placed = (
        P(("dp", "tensor"), None),
        P("dp"),
        P(None, ("dp", "tensor")),
        P(("dp", "tensor")),
        P(None, "dp", "tensor"),
        P("tensor", "dp"),
        P("dp", "tensor"),
        P("tensor", "dp"),
        P(("dp", "tensor"), None),
    )
    return jax.shard_map(
        on_device,
        mesh=mesh,
        in_specs=placed,
        out_specs=(
            P(("dp", "tensor"), None),
            P(("dp", "tensor"), None),
            P(None, ("dp", "tensor")),
            P(("dp", "tensor")),
            P(None, "dp", "tensor"),
            P("tensor", "dp"),
            P("dp", "tensor"),
            P("tensor", "dp"),
        ),
        check_vma=False,
    )
```

```python
import functools

import jax
import jax.numpy as jnp
from jax import lax
from jax.experimental import pallas as pl
from jax.experimental.pallas import tpu as pltpu
from jax.sharding import PartitionSpec as P

HEAD_DIM = 64


EPSILON = 1e-06
NEGATIVE = -1e30
MESH = pl.DeviceIdType.MESH
LANES = 128


def peer_at(axis, k):
    if axis == "all":
        dp, tensor = lax.axis_size("dp"), lax.axis_size("tensor")
        index = lax.rem(lax.axis_index("dp") * tensor + lax.axis_index("tensor") + k, dp * tensor)
        return index, {"dp": index // tensor, "tensor": lax.rem(index, tensor)}
    index = lax.rem(lax.axis_index(axis) + k, lax.axis_size(axis))
    return index, {axis: index}


def my_index(axis):
    if axis == "all":
        return lax.axis_index("dp") * lax.axis_size("tensor") + lax.axis_index("tensor")
    return lax.axis_index(axis)


def size_of(axis):
    if axis == "all":
        return lax.axis_size("dp") * lax.axis_size("tensor")
    return lax.axis_size(axis)


def view(ref, spot, index):
    if spot is None:
        return ref.at[index]
    dim, width = spot
    place = pl.ds(pl.multiple_of(index * width, width), width)
    return ref.at[tuple([slice(None)] * dim + [place])]


def for_each(count, body):
    lax.fori_loop(0, count, lambda k, carry: (body(k), carry)[1], 0)


class Task:
    place = pl.ANY

    def step(self, number, src, out, sems):
        pass


class Gather(Task):
    def __init__(self, axis, block, spot=None):
        self.axis, self.array, self.spot = axis, block, spot
        shape = list(block.shape)
        if spot is None:
            shape = [size_of(axis)] + shape
        else:
            shape[spot[0]] *= size_of(axis)
        self.out = jax.ShapeDtypeStruct(tuple(shape), block.dtype)
        self.sems = [
            pltpu.SemaphoreType.DMA((size_of(axis),)),
            pltpu.SemaphoreType.DMA((size_of(axis),)),
            pltpu.SemaphoreType.DMA,
        ]

    def own(self, src, out, sems):
        return pltpu.make_async_copy(src, view(out, self.spot, my_index(self.axis)), sems[2])

    def copy(self, src, out, sems, k):
        _, device = peer_at(self.axis, k)
        mine = view(out, self.spot, my_index(self.axis))
        return pltpu.make_async_remote_copy(
            src, mine, sems[0].at[k], sems[1].at[k], device_id=device, device_id_type=MESH
        )

    def start(self, src, out, sems):
        for_each(size_of(self.axis) - 1, lambda k: self.copy(src, out, sems, k + 1).start())
        self.own(src, out, sems).start()

    def finish(self, src, out, sems):
        for_each(size_of(self.axis) - 1, lambda k: self.copy(src, out, sems, k + 1).wait())
        self.own(src, out, sems).wait()


class PairGather(Gather):
    def __init__(self, block, spot=None):
        super().__init__("dp", block, spot)
        half = size_of("dp") // 2
        self.sems = [pltpu.SemaphoreType.DMA((half,)) for _ in range(4)]
        self.sems.append(pltpu.SemaphoreType.DMA)

    def own(self, src, out, sems):
        return pltpu.make_async_copy(src, view(out, self.spot, my_index("dp")), sems[4])

    def away(self, src, out, sems, k):
        _, device = peer_at("dp", 2 * k)
        mine = view(out, self.spot, my_index("dp"))
        return pltpu.make_async_remote_copy(
            src, mine, sems[0].at[k], sems[1].at[k], device_id=device, device_id_type=MESH
        )

    def share(self, src, out, sems, k, first=False):
        count = size_of("dp")
        me = my_index("dp")
        place = view(out, self.spot, lax.rem(me - 2 * k + count, count))
        return pltpu.make_async_remote_copy(
            src if first else place,
            place,
            sems[2].at[k],
            sems[3].at[k],
            device_id={"dp": me + 1 - 2 * lax.rem(me, 2)},
            device_id_type=MESH,
        )

    def start(self, src, out, sems):
        for_each(size_of("dp") // 2 - 1, lambda k: self.away(src, out, sems, k + 1).start())
        self.share(src, out, sems, 0, True).start()
        self.own(src, out, sems).start()

    def step(self, number, src, out, sems):
        if number != size_of("tensor") - 1:
            return

        def pass_on(k):
            self.away(src, out, sems, k + 1).wait_recv()
            self.share(src, out, sems, k + 1).start()

        for_each(size_of("dp") // 2 - 1, pass_on)

    def finish(self, src, out, sems):
        for_each(size_of("dp") // 2 - 1, lambda k: self.away(src, out, sems, k + 1).wait_send())
        self.share(src, out, sems, 0, True).wait()
        for_each(size_of("dp") // 2 - 1, lambda k: self.share(src, out, sems, k + 1).wait())
        self.own(src, out, sems).wait()


class Swap(Task):
    def __init__(self, axis, array, spot=None):
        self.axis, self.array, self.spot = axis, array, spot
        shape = list(array.shape)
        if spot is None:
            shape = shape[1:]
        else:
            shape[spot[0]] = spot[1]
        self.out = jax.ShapeDtypeStruct((size_of(axis) - 1, *shape), array.dtype)
        self.sems = [pltpu.SemaphoreType.DMA((size_of(axis),)) for _ in range(2)]

    def copy(self, src, out, sems, k):
        index, device = peer_at(self.axis, k)
        return pltpu.make_async_remote_copy(
            view(src, self.spot, index),
            out.at[k - 1],
            sems[0].at[k],
            sems[1].at[k],
            device_id=device,
            device_id_type=MESH,
        )

    def start(self, src, out, sems):
        for_each(size_of(self.axis) - 1, lambda k: self.copy(src, out, sems, k + 1).start())

    def finish(self, src, out, sems):
        for_each(size_of(self.axis) - 1, lambda k: self.copy(src, out, sems, k + 1).wait())


class PairSwap(Task):
    axis = "dp"
    place = pltpu.VMEM

    def __init__(self, array, spot=None):
        self.array, self.spot = array, spot
        shape = list(array.shape)
        if spot is None:
            shape = shape[1:]
        else:
            shape[spot[0]] = spot[1]
        half = size_of("dp") // 2
        self.out = jax.ShapeDtypeStruct((half, *shape), array.dtype)
        self.sems = [pltpu.SemaphoreType.DMA((half,)) for _ in range(4)]
        self.sems.append(pltpu.VMEM((half, *shape), array.dtype))

    def share(self, src, dst, sems, k):
        me = my_index("dp")
        partner = me + 1 - 2 * lax.rem(me, 2)
        return pltpu.make_async_remote_copy(
            view(src, self.spot, lax.rem(partner + 2 * k, size_of("dp"))),
            dst.at[k],
            sems[0].at[k],
            sems[1].at[k],
            device_id={"dp": partner},
            device_id_type=MESH,
        )

    def away(self, out, sems, k):
        _, device = peer_at("dp", 2 * k)
        return pltpu.make_async_remote_copy(
            sems[4].at[k],
            out.at[k],
            sems[2].at[k],
            sems[3].at[k],
            device_id=device,
            device_id_type=MESH,
        )

    def start(self, src, out, sems):
        others = size_of("dp") // 2 - 1
        for_each(others, lambda k: self.share(src, sems[4], sems, k + 1).start())
        self.share(src, out, sems, 0).start()

    def step(self, number, src, out, sems):
        if number != 1:
            return

        def pass_on(k):
            self.share(src, sems[4], sems, k).wait_recv()
            index, _ = peer_at("dp", 2 * k)
            own = view(src, self.spot, index)[...].astype(jnp.float32)
            sems[4][k] = (sems[4][k].astype(jnp.float32) + own).astype(src.dtype)
            self.away(out, sems, k).start()

        for_each(size_of("dp") // 2 - 1, lambda k: pass_on(k + 1))

    def finish(self, src, out, sems):
        others = size_of("dp") // 2 - 1
        for_each(others, lambda k: self.share(src, sems[4], sems, k + 1).wait_send())
        self.share(src, out, sems, 0).wait()
        for_each(others, lambda k: self.away(out, sems, k + 1).wait())


class Line(Task):
    axis = "tensor"

    def remote(self, src, dst, sems, way, index):
        target = lax.axis_index("tensor") + (1 - 2 * way)
        return pltpu.make_async_remote_copy(
            src,
            dst,
            sems[0].at[way, index],
            sems[1].at[way, index],
            device_id={"tensor": target},
            device_id_type=MESH,
        )


class LineGather(Line):
    def __init__(self, block):
        self.array = block
        count = size_of("tensor")
        self.out = jax.ShapeDtypeStruct((count, *block.shape), block.dtype)
        self.sems = [
            pltpu.SemaphoreType.DMA((2, count)),
            pltpu.SemaphoreType.DMA((2, count)),
            pltpu.SemaphoreType.DMA,
        ]

    def own(self, src, out, sems):
        return pltpu.make_async_copy(src, out.at[lax.axis_index("tensor")], sems[2])

    def start(self, src, out, sems):
        me, last = lax.axis_index("tensor"), size_of("tensor") - 1
        pl.when(me < last)(lambda: self.remote(src, out.at[me], sems, 0, me).start())
        pl.when(me > 0)(lambda: self.remote(src, out.at[me], sems, 1, me).start())
        self.own(src, out, sems).start()

    def step(self, number, src, out, sems):
        me, last = lax.axis_index("tensor"), size_of("tensor") - 1
        for way, index, here, more in (
            (0, me - number, me >= number, me < last),
            (1, me + number, me + number <= last, me > 0),
        ):

            @pl.when(here)
            def _():
                copy = self.remote(out.at[index], out.at[index], sems, way, index)
                copy.wait_recv()
                pl.when(more)(copy.start)

    def finish(self, src, out, sems):
        me, last = lax.axis_index("tensor"), size_of("tensor") - 1
        for number in range(last + 1):
            for way, index, sent in (
                (0, me - number, (me >= number) & (me < last)),
                (1, me + number, (me + number <= last) & (me > 0)),
            ):
                copy = self.remote(src, out.at[me], sems, way, index)
                pl.when(sent)(copy.wait_send)
        self.own(src, out, sems).wait()


class LineSum(Line):
    place = pltpu.VMEM

    def __init__(self, blocks):
        self.array = blocks
        count = blocks.shape[0]
        self.out = jax.ShapeDtypeStruct((2, *blocks.shape[1:]), blocks.dtype)
        self.sems = [
            pltpu.SemaphoreType.DMA((2, count)),
            pltpu.SemaphoreType.DMA((2, count)),
            pltpu.VMEM((2, *blocks.shape), blocks.dtype),
        ]

    def start(self, src, out, sems):
        self.move(0, src, sems)

    def step(self, number, src, out, sems):
        if number < size_of("tensor") - 1:
            self.move(number, src, sems)

    def routes(self, number):
        me, last = lax.axis_index("tensor"), size_of("tensor") - 1
        up, down = number - me, number - (last - me)
        return (
            (0, last - up, (up >= 0) & (last - up > me), me > 0),
            (1, down, (down >= 0) & (down < me), me < last),
        )

    def move(self, number, src, sems):
        held = sems[2]
        for way, index, sends, follows in self.routes(number):

            @pl.when(sends)
            def _():
                slot = held.at[way, index]

                @pl.when(follows)
                def _():
                    self.remote(slot, slot, sems, way, index).wait_recv()
                    self.add(src, held, way, index)
                    self.remote(slot, slot, sems, way, index).start()

                @pl.when(jnp.logical_not(follows))
                def _():
                    if number > 0:
                        before = index + 1 - 2 * way
                        self.remote(slot, slot, sems, way, before).wait_send()
                    self.remote(src.at[index], slot, sems, way, index).start()

    def add(self, src, held, way, index):
        width = 2 * LANES
        for at in range(0, held.shape[3], width):
            part = held[way, index, :, at : at + width].astype(jnp.float32)
            part += src[index, :, at : at + width].astype(jnp.float32)
            held[way, index, :, at : at + width] = part.astype(held.dtype)

    def finish(self, src, out, sems):
        me, last = lax.axis_index("tensor"), size_of("tensor") - 1
        held = sems[2]
        for way, comes in ((0, me > 0), (1, me < last)):

            @pl.when(comes)
            def _():
                slot = held.at[way, me]
                self.remote(slot, slot, sems, way, me).wait_recv()
                out[way] = held[way, me]

            @pl.when(jnp.logical_not(comes))
            def _():
                out[way] = jnp.zeros(out.shape[1:], out.dtype)

        for number in range(last):
            for way, index, sends, follows in self.routes(number):
                slot = held.at[way, index]
                waits = sends if number == last - 1 else sends & follows
                pl.when(waits)(self.remote(slot, slot, sems, way, index).wait_send)


def padded_bytes(array):
    *lead, rows, columns = array.shape
    size = -(-rows // 16) * 16 * -(-columns // LANES) * LANES * array.dtype.itemsize
    for extent in lead:
        size *= extent
    return size


def held_bytes(tasks):
    total = 6 * 2**20
    for task in tasks:
        if task.place is not pl.ANY:
            total += padded_bytes(task.array) + 2 * padded_bytes(task.out)
            total += 2 * padded_bytes(task.array) if isinstance(task, LineSum) else 0
    return total


def exchange(number, *tasks):
    axes = sorted({task.axis for task in tasks})
    if "all" in axes:
        axes = ["all"]
    count = len(tasks)

    def kernel(*refs):
        sources, outs, sems = refs[:count], refs[count : 2 * count], list(refs[2 * count :])
        grouped = []
        for task in tasks:
            grouped.append([sems.pop(0) for _ in task.sems])
        barrier = pltpu.get_barrier_semaphore()

        def greet(axis, k):
            _, device = peer_at(axis, k)
            pl.semaphore_signal(barrier, inc=1, device_id=device, device_id_type=MESH)

        for axis in axes:
            for_each(size_of(axis) - 1, functools.partial(lambda a, k: greet(a, k + 1), axis))
        pl.semaphore_wait(barrier, sum(size_of(axis) - 1 for axis in axes))
        every = list(zip(tasks, sources, outs, grouped))
        for task, src, out, own in every:
            task.start(src, out, own)
        by_wait = sorted(every, key=lambda entry: isinstance(entry[0], Line))
        for step in range(1, size_of("tensor")):
            for task, src, out, own in by_wait:
                task.step(step, src, out, own)
        for task, src, out, own in every:
            task.finish(src, out, own)

    return pl.pallas_call(
        kernel,
        out_shape=[task.out for task in tasks],
        in_specs=[pl.BlockSpec(memory_space=task.place) for task in tasks],
        out_specs=[pl.BlockSpec(memory_space=task.place) for task in tasks],
        scratch_shapes=[sem for task in tasks for sem in task.sems],
        compiler_params=pltpu.CompilerParams(
            collective_id=number, has_side_effects=True, vmem_limit_bytes=held_bytes(tasks)
        ),
    )(*[task.array for task in tasks])


def spot_of(block, dim, width):
    grain = LANES if dim == block.ndim - 1 else 16
    return (dim, width) if width % grain == 0 else None


def weight_gather(block, dim):
    return PairGather(block, spot_of(block, dim, block.shape[dim]))


def joined(gathered, block, dim):
    if gathered.ndim == block.ndim:
        return gathered
    moved = jnp.moveaxis(gathered, 0, dim)
    shape = list(block.shape)
    shape[dim] *= gathered.shape[0]
    return moved.reshape(shape)


def grad_swap(term, dim):
    count = size_of("dp")
    width = term.shape[dim] // count
    low = term.astype(jnp.bfloat16)
    spot = spot_of(low, dim, width)
    if spot is None:
        shape = list(low.shape)
        shape[dim : dim + 1] = [count, width]
        low = jnp.moveaxis(low.reshape(shape), dim, 0)
    return PairSwap(low, spot)


def own_part(term, axis, dim):
    width = term.shape[dim] // size_of(axis)
    return lax.dynamic_slice_in_dim(term, my_index(axis) * width, width, dim)


def summed(own, others):
    return own + jnp.sum(others.astype(jnp.float32), axis=0)


def normalized(values):
    centred = values - jnp.mean(values, axis=-1, keepdims=True)
    spread = jnp.mean(centred * centred, axis=-1, keepdims=True)
    return centred * lax.rsqrt(spread + EPSILON)


def layer_norm(values, gain, shift):
    return normalized(values) * gain + shift


def exact_gelu(values):
    return jax.nn.gelu(values, approximate=False)


def dot(left, right, left_dim, right_dim):
    dims = (((left_dim,), (right_dim,)), ((), ()))
    return lax.dot_general(left, right, dims, preferred_element_type=jnp.float32)


def head_columns(ref, part, head, width):
    start = part * width + head * HEAD_DIM
    return ref[:, start : start + HEAD_DIM]


def attend_kernel(scale, qkv, mask, mixed, log_total):
    width = mixed.shape[1]
    for head in range(width // HEAD_DIM):
        query, keys, values = [head_columns(qkv, part, head, width) for part in range(3)]
        scores = jnp.where(mask[0:1, :] > 0, dot(query, keys, 1, 1) * scale, NEGATIVE)
        largest = jnp.max(scores, axis=-1, keepdims=True)
        powers = jnp.exp(scores - largest)
        total = jnp.sum(powers, axis=-1, keepdims=True)
        probs = (powers * (1.0 / total)).astype(jnp.bfloat16)
        columns = slice(head * HEAD_DIM, (head + 1) * HEAD_DIM)
        mixed[:, columns] = dot(probs, values, 1, 0).astype(jnp.bfloat16)
        log_total[:, head : head + 1] = largest + jnp.log(total)


def attend_back_kernel(scale, qkv, mask, log_total, grad_mixed, grads):
    width = grad_mixed.shape[1]
    for head in range(width // HEAD_DIM):
        query, keys, values = [head_columns(qkv, part, head, width) for part in range(3)]
        grad = head_columns(grad_mixed, 0, head, width)
        scores = jnp.where(mask[0:1, :] > 0, dot(query, keys, 1, 1) * scale, NEGATIVE)
        probs = jnp.exp(scores - log_total[:, head : head + 1])
        grad_probs = dot(grad, values, 1, 1)
        inner = jnp.sum(grad_probs * probs, axis=-1, keepdims=True)
        grad_scores = (probs * (grad_probs - inner)).astype(jnp.bfloat16)
        results = (
            dot(grad_scores, keys, 1, 0) * scale,
            dot(grad_scores, query, 0, 0) * scale,
            dot(probs.astype(jnp.bfloat16), grad, 0, 0),
        )
        for part, result in enumerate(results):
            start = part * width + head * HEAD_DIM
            grads[:, start : start + HEAD_DIM] = result.astype(jnp.bfloat16)


def in_vmem(kernel, outs, *arrays):
    return pl.pallas_call(
        kernel,
        out_shape=outs,
        in_specs=[pl.BlockSpec(memory_space=pltpu.VMEM)] * len(arrays),
        out_specs=[pl.BlockSpec(memory_space=pltpu.VMEM)] * len(outs),
        compiler_params=pltpu.CompilerParams(vmem_limit_bytes=32 * 2**20),
    )(*arrays)


def row_validity(counts, seq, rows):
    places = jnp.arange(rows, dtype=jnp.int32)
    owner = places // seq
    position = places - owner * seq
    picks = owner[:, None] == jnp.arange(counts.shape[0], dtype=jnp.int32)[None, :]
    return position < jnp.sum(jnp.where(picks, counts[None, :], 0), axis=1)


def row_sum(part, rows):
    return LineSum(part.astype(jnp.bfloat16).reshape(-1, rows, part.shape[1]))


def row_permutes(part, rows):
    count = size_of("tensor")
    parts = part.reshape(count, rows, part.shape[1])
    others = []
    for k in range(1, count):
        index, _ = peer_at("tensor", k)
        block = lax.dynamic_index_in_dim(parts, index, 0, keepdims=False)
        pairs = [(i, (i + k) % count) for i in range(count)]
        others.append(lax.ppermute(block, "tensor", pairs))
    return others


def on_device(tokens, counts, vectors, fc1_bias, w_qkv, w_out, w_fc1, w_fc2, cotangent):
    tensor_count = lax.axis_size("tensor")
    tensor_index = lax.axis_index("tensor")
    devices = size_of("all")
    model_width = tokens.shape[1]
    vector_size = vectors.size
    small_size = vector_size + fc1_bias.size
    small_rows = -(-small_size // (8 * LANES)) * 8
    small = jnp.concatenate([vectors.reshape(-1), fc1_bias])
    small = jnp.pad(small, (0, small_rows * LANES - small_size)).reshape(small_rows, LANES)
    local_rows = tokens.shape[0]
    block_rows = local_rows * tensor_count
    images = counts.shape[0]
    local_valid = row_validity(counts, block_rows // images, block_rows)
    local_valid = lax.dynamic_slice_in_dim(local_valid, tensor_index * local_rows, local_rows)
    local_valid = local_valid.astype(jnp.float32)[:, None]
    masked_out = local_valid * cotangent
    width = w_qkv.shape[2]
    w_qkv_flat = w_qkv.transpose(1, 0, 2).reshape(w_qkv.shape[1], 3 * width)
    small_all, unscaled, gathered_grad, qkv_all, out_all, fc1_all, fc2_all = exchange(
        0,
        Gather("all", small),
        LineGather(normalized(tokens).astype(jnp.bfloat16)),
        LineGather(masked_out.astype(jnp.bfloat16)),
        weight_gather(w_qkv_flat, 0),
        weight_gather(w_out, 1),
        weight_gather(w_fc1, 0),
        weight_gather(w_fc2, 1),
    )
    qkv_all = joined(qkv_all, w_qkv_flat, 0)
    out_all = joined(out_all, w_out, 1)
    fc1_all = joined(fc1_all, w_fc1, 0)
    fc2_all = joined(fc2_all, w_fc2, 1)
    gathered_grad = gathered_grad.reshape(block_rows, model_width)
    small_all = small_all.reshape(devices, small_rows * LANES)
    full_vectors = small_all[:, :vector_size].reshape(devices, vectors.shape[0], -1)
    full_vectors = full_vectors.transpose(1, 0, 2).reshape(vectors.shape[0], model_width)
    full_fc1 = small_all[:, vector_size:small_size].reshape(-1)
    unscaled = unscaled.reshape(block_rows, model_width).astype(jnp.float32)
    gathered = (unscaled * full_vectors[0] + full_vectors[1]).astype(jnp.bfloat16)
    seq = block_rows // images
    hidden_width = w_fc1.shape[1]
    heads_local = width // HEAD_DIM
    scale = HEAD_DIM ** (-0.5)
    block_valid = row_validity(counts, seq, block_rows)
    query_bias = lax.dynamic_slice_in_dim(full_vectors[2], tensor_index * width, width)
    value_bias = lax.dynamic_slice_in_dim(full_vectors[3], tensor_index * width, width)
    hidden_bias = lax.dynamic_slice_in_dim(full_fc1, tensor_index * hidden_width, hidden_width)
    qkv_bias = jnp.concatenate([query_bias, jnp.zeros_like(query_bias), value_bias])
    projected = jnp.dot(gathered, qkv_all, preferred_element_type=jnp.float32)
    qkv = (projected + qkv_bias).astype(jnp.bfloat16)
    mask = jnp.broadcast_to(block_valid.astype(jnp.float32), (8, block_rows))
    mixed_all, log_total = in_vmem(
        functools.partial(attend_kernel, scale),
        [
            jax.ShapeDtypeStruct((block_rows, width), jnp.bfloat16),
            jax.ShapeDtypeStruct((block_rows, heads_local), jnp.float32),
        ],
        qkv,
        mask,
    )
    attn_part = jnp.dot(mixed_all, out_all, preferred_element_type=jnp.float32)
    (attn_others,) = exchange(1, row_sum(attn_part, local_rows))
    attn_local = summed(own_part(attn_part, "tensor", 0), attn_others)
    middle = tokens + local_valid * (attn_local + full_vectors[4])
    normed2 = layer_norm(middle, full_vectors[5], full_vectors[6]).astype(jnp.bfloat16)
    (gathered2,) = exchange(2, LineGather(normed2))
    gathered2 = gathered2.reshape(block_rows, model_width)
    pre = jnp.dot(gathered2, fc1_all, preferred_element_type=jnp.float32) + hidden_bias
    hidden_float, gelu_back = jax.vjp(exact_gelu, pre)
    hidden = hidden_float.astype(jnp.bfloat16)
    mlp_part = jnp.dot(hidden, fc2_all, preferred_element_type=jnp.float32)
    grad_shift2 = jnp.sum(masked_out, axis=0)
    fc2_term = jnp.einsum("rf,rd->fd", hidden, gathered_grad, preferred_element_type=jnp.float32)
    grad_hidden = jnp.einsum(
        "rd,fd->rf", gathered_grad, fc2_all, preferred_element_type=jnp.float32
    )
    grad_pre = gelu_back(grad_hidden)[0].astype(jnp.bfloat16)
    hidden_bias_grad = jnp.sum(grad_pre.astype(jnp.float32), axis=0)
    fc1_term = jnp.einsum("rd,rf->df", gathered2, grad_pre, preferred_element_type=jnp.float32)
    normed2_part = jnp.einsum("rf,df->rd", grad_pre, fc1_all, preferred_element_type=jnp.float32)
    normed2_others, fc2_others = exchange(
        3, row_sum(normed2_part, local_rows), grad_swap(fc2_term, 1)
    )
    grad_normed2 = summed(own_part(normed2_part, "tensor", 0), normed2_others)
    fc2_grad = summed(own_part(fc2_term, "dp", 1), fc2_others)
    second_norm, second_back = jax.vjp(layer_norm, middle, full_vectors[5], full_vectors[6])
    grad_through, gain2_grad, shift2_grad = second_back(grad_normed2)
    grad_middle = cotangent + grad_through
    masked_middle = local_valid * grad_middle
    out_bias_grad = jnp.sum(masked_middle, axis=0)
    gathered_attn, fc1_others = exchange(
        4, LineGather(masked_middle.astype(jnp.bfloat16)), grad_swap(fc1_term, 0)
    )
    fc1_grad = summed(own_part(fc1_term, "dp", 0), fc1_others)
    gathered_attn, mlp_low = lax.optimization_barrier(
        (gathered_attn, mlp_part.astype(jnp.bfloat16))
    )
    mlp_others = row_permutes(mlp_low, local_rows)
    mlp_local = own_part(mlp_part, "tensor", 0)
    for block in mlp_others:
        mlp_local = mlp_local + block.astype(jnp.float32)
    layer_out = middle + local_valid * (mlp_local + full_vectors[7])
    gathered_attn = gathered_attn.reshape(block_rows, model_width)
    out_term = jnp.einsum("re,rd->ed", mixed_all, gathered_attn, preferred_element_type=jnp.float32)
    grad_mixed = jnp.einsum("rd,ed->re", gathered_attn, out_all, preferred_element_type=jnp.float32)
    (qkv_back,) = in_vmem(
        functools.partial(attend_back_kernel, scale),
        [jax.ShapeDtypeStruct(qkv.shape, jnp.bfloat16)],
        qkv,
        mask,
        log_total,
        grad_mixed.astype(jnp.bfloat16),
    )
    qkv_bias_grad = jnp.sum(qkv_back.astype(jnp.float32), axis=0)
    query_bias_grad, value_bias_grad = qkv_bias_grad[:width], qkv_bias_grad[2 * width :]
    qkv_term = jnp.einsum("rd,re->de", gathered, qkv_back, preferred_element_type=jnp.float32)
    normed_part = jnp.einsum("re,de->rd", qkv_back, qkv_all, preferred_element_type=jnp.float32)
    gain1_grad = jnp.sum(normed_part * unscaled, axis=0)
    shift1_grad = jnp.sum(normed_part, axis=0)
    zeros_model = jnp.zeros((model_width,), jnp.float32)
    query_bias_full = lax.dynamic_update_slice_in_dim(
        zeros_model, query_bias_grad, tensor_index * width, 0
    )
    value_bias_full = lax.dynamic_update_slice_in_dim(
        zeros_model, value_bias_grad, tensor_index * width, 0
    )
    vector_terms = jnp.stack(
        [
            gain1_grad,
            shift1_grad,
            query_bias_full,
            value_bias_full,
            out_bias_grad,
            gain2_grad,
            shift2_grad,
            grad_shift2,
        ]
    )
    zeros_hidden = jnp.zeros((full_fc1.shape[0],), jnp.float32)
    hidden_bias_full = lax.dynamic_update_slice_in_dim(
        zeros_hidden, hidden_bias_grad, tensor_index * hidden_width, 0
    )
    vector_blocks = vector_terms.reshape(vectors.shape[0], devices, -1).transpose(1, 0, 2)
    small_terms = jnp.concatenate(
        [vector_blocks.reshape(devices, -1), hidden_bias_full.reshape(devices, -1)], axis=1
    )
    small_terms = jnp.pad(small_terms, ((0, 0), (0, small_rows * LANES - small_size)))
    small_terms = small_terms.reshape(devices, small_rows, LANES)
    normed_others, qkv_others, out_others, small_others = exchange(
        5,
        row_sum(normed_part, local_rows),
        grad_swap(qkv_term, 0),
        grad_swap(out_term, 1),
        Swap("all", small_terms),
    )
    grad_normed = summed(own_part(normed_part, "tensor", 0), normed_others)
    qkv_grad = summed(own_part(qkv_term, "dp", 0), qkv_others)
    qkv_grad = qkv_grad.reshape(-1, 3, width).transpose(1, 0, 2)
    out_grad = summed(own_part(out_term, "dp", 1), out_others)
    first_norm, first_back = jax.vjp(layer_norm, tokens, full_vectors[0], full_vectors[1])
    grad_input_norm, _, _ = first_back(grad_normed)
    input_grad = grad_middle + grad_input_norm
    small_grad = summed(own_part(small_terms, "all", 0)[0], small_others).reshape(-1)
    vectors_grad = small_grad[:vector_size].reshape(vectors.shape)
    fc1_bias_grad = small_grad[vector_size:small_size]
    return (
        layer_out,
        input_grad,
        vectors_grad,
        fc1_bias_grad,
        qkv_grad,
        out_grad,
        fc1_grad,
        fc2_grad,
    )


def solution(mesh):
    placed = (
        P(("dp", "tensor"), None),
        P("dp"),
        P(None, ("dp", "tensor")),
        P(("dp", "tensor")),
        P(None, "dp", "tensor"),
        P("tensor", "dp"),
        P("dp", "tensor"),
        P("tensor", "dp"),
        P(("dp", "tensor"), None),
    )
    return jax.shard_map(
        on_device,
        mesh=mesh,
        in_specs=placed,
        out_specs=(
            P(("dp", "tensor"), None),
            P(("dp", "tensor"), None),
            P(None, ("dp", "tensor")),
            P(("dp", "tensor")),
            P(None, "dp", "tensor"),
            P("tensor", "dp"),
            P("dp", "tensor"),
            P("tensor", "dp"),
        ),
        check_vma=False,
    )
```

```python
import functools

import jax
import jax.numpy as jnp
from jax import lax
from jax.experimental import pallas as pl
from jax.experimental.pallas import tpu as pltpu
from jax.sharding import PartitionSpec as P

HEAD_DIM = 64


EPSILON = 1e-06
NEGATIVE = -1e30
MESH = pl.DeviceIdType.MESH
LANES = 128


def peer_at(axis, k):
    if axis == "all":
        dp, tensor = lax.axis_size("dp"), lax.axis_size("tensor")
        index = lax.rem(lax.axis_index("dp") * tensor + lax.axis_index("tensor") + k, dp * tensor)
        return index, {"dp": index // tensor, "tensor": lax.rem(index, tensor)}
    index = lax.rem(lax.axis_index(axis) + k, lax.axis_size(axis))
    return index, {axis: index}


def my_index(axis):
    if axis == "all":
        return lax.axis_index("dp") * lax.axis_size("tensor") + lax.axis_index("tensor")
    return lax.axis_index(axis)


def size_of(axis):
    if axis == "all":
        return lax.axis_size("dp") * lax.axis_size("tensor")
    return lax.axis_size(axis)


def view(ref, spot, index):
    if spot is None:
        return ref.at[index]
    dim, width = spot
    place = pl.ds(pl.multiple_of(index * width, width), width)
    return ref.at[tuple([slice(None)] * dim + [place])]


def for_each(count, body):
    lax.fori_loop(0, count, lambda k, carry: (body(k), carry)[1], 0)


class Task:
    place = pl.ANY

    def step(self, number, src, out, sems):
        pass


class Gather(Task):
    def __init__(self, axis, block, spot=None):
        self.axis, self.array, self.spot = axis, block, spot
        shape = list(block.shape)
        if spot is None:
            shape = [size_of(axis)] + shape
        else:
            shape[spot[0]] *= size_of(axis)
        self.out = jax.ShapeDtypeStruct(tuple(shape), block.dtype)
        self.sems = [
            pltpu.SemaphoreType.DMA((size_of(axis),)),
            pltpu.SemaphoreType.DMA((size_of(axis),)),
            pltpu.SemaphoreType.DMA,
        ]

    def own(self, src, out, sems):
        return pltpu.make_async_copy(src, view(out, self.spot, my_index(self.axis)), sems[2])

    def copy(self, src, out, sems, k):
        _, device = peer_at(self.axis, k)
        mine = view(out, self.spot, my_index(self.axis))
        return pltpu.make_async_remote_copy(
            src, mine, sems[0].at[k], sems[1].at[k], device_id=device, device_id_type=MESH
        )

    def start(self, src, out, sems):
        for_each(size_of(self.axis) - 1, lambda k: self.copy(src, out, sems, k + 1).start())
        self.own(src, out, sems).start()

    def finish(self, src, out, sems):
        for_each(size_of(self.axis) - 1, lambda k: self.copy(src, out, sems, k + 1).wait())
        self.own(src, out, sems).wait()


class PairGather(Gather):
    def __init__(self, block, spot=None):
        super().__init__("dp", block, spot)
        half = size_of("dp") // 2
        self.sems = [pltpu.SemaphoreType.DMA((half,)) for _ in range(4)]
        self.sems.append(pltpu.SemaphoreType.DMA)

    def own(self, src, out, sems):
        return pltpu.make_async_copy(src, view(out, self.spot, my_index("dp")), sems[4])

    def away(self, src, out, sems, k):
        _, device = peer_at("dp", 2 * k)
        mine = view(out, self.spot, my_index("dp"))
        return pltpu.make_async_remote_copy(
            src, mine, sems[0].at[k], sems[1].at[k], device_id=device, device_id_type=MESH
        )

    def share(self, src, out, sems, k, first=False):
        count = size_of("dp")
        me = my_index("dp")
        place = view(out, self.spot, lax.rem(me - 2 * k + count, count))
        return pltpu.make_async_remote_copy(
            src if first else place,
            place,
            sems[2].at[k],
            sems[3].at[k],
            device_id={"dp": me + 1 - 2 * lax.rem(me, 2)},
            device_id_type=MESH,
        )

    def start(self, src, out, sems):
        for_each(size_of("dp") // 2 - 1, lambda k: self.away(src, out, sems, k + 1).start())
        self.share(src, out, sems, 0, True).start()
        self.own(src, out, sems).start()

    def step(self, number, src, out, sems):
        if number != size_of("tensor") - 1:
            return

        def pass_on(k):
            self.away(src, out, sems, k + 1).wait_recv()
            self.share(src, out, sems, k + 1).start()

        for_each(size_of("dp") // 2 - 1, pass_on)

    def finish(self, src, out, sems):
        for_each(size_of("dp") // 2 - 1, lambda k: self.away(src, out, sems, k + 1).wait_send())
        self.share(src, out, sems, 0, True).wait()
        for_each(size_of("dp") // 2 - 1, lambda k: self.share(src, out, sems, k + 1).wait())
        self.own(src, out, sems).wait()


class Swap(Task):
    def __init__(self, axis, array, spot=None):
        self.axis, self.array, self.spot = axis, array, spot
        shape = list(array.shape)
        if spot is None:
            shape = shape[1:]
        else:
            shape[spot[0]] = spot[1]
        self.out = jax.ShapeDtypeStruct((size_of(axis) - 1, *shape), array.dtype)
        self.sems = [pltpu.SemaphoreType.DMA((size_of(axis),)) for _ in range(2)]

    def copy(self, src, out, sems, k):
        index, device = peer_at(self.axis, k)
        return pltpu.make_async_remote_copy(
            view(src, self.spot, index),
            out.at[k - 1],
            sems[0].at[k],
            sems[1].at[k],
            device_id=device,
            device_id_type=MESH,
        )

    def start(self, src, out, sems):
        for_each(size_of(self.axis) - 1, lambda k: self.copy(src, out, sems, k + 1).start())

    def finish(self, src, out, sems):
        for_each(size_of(self.axis) - 1, lambda k: self.copy(src, out, sems, k + 1).wait())


class PairSwap(Task):
    axis = "dp"
    place = pltpu.VMEM

    def __init__(self, array, spot=None):
        self.array, self.spot = array, spot
        shape = list(array.shape)
        if spot is None:
            shape = shape[1:]
        else:
            shape[spot[0]] = spot[1]
        half = size_of("dp") // 2
        self.out = jax.ShapeDtypeStruct((half, *shape), array.dtype)
        self.sems = [pltpu.SemaphoreType.DMA((half,)) for _ in range(4)]
        self.sems.append(pltpu.VMEM((half, *shape), array.dtype))

    def share(self, src, dst, sems, k):
        me = my_index("dp")
        partner = me + 1 - 2 * lax.rem(me, 2)
        return pltpu.make_async_remote_copy(
            view(src, self.spot, lax.rem(partner + 2 * k, size_of("dp"))),
            dst.at[k],
            sems[0].at[k],
            sems[1].at[k],
            device_id={"dp": partner},
            device_id_type=MESH,
        )

    def away(self, out, sems, k):
        _, device = peer_at("dp", 2 * k)
        return pltpu.make_async_remote_copy(
            sems[4].at[k],
            out.at[k],
            sems[2].at[k],
            sems[3].at[k],
            device_id=device,
            device_id_type=MESH,
        )

    def start(self, src, out, sems):
        others = size_of("dp") // 2 - 1
        for_each(others, lambda k: self.share(src, sems[4], sems, k + 1).start())
        self.share(src, out, sems, 0).start()

    def step(self, number, src, out, sems):
        if number != 1:
            return

        def pass_on(k):
            self.share(src, sems[4], sems, k).wait_recv()
            index, _ = peer_at("dp", 2 * k)
            own = view(src, self.spot, index)[...].astype(jnp.float32)
            sems[4][k] = (sems[4][k].astype(jnp.float32) + own).astype(src.dtype)
            self.away(out, sems, k).start()

        for_each(size_of("dp") // 2 - 1, lambda k: pass_on(k + 1))

    def finish(self, src, out, sems):
        others = size_of("dp") // 2 - 1
        for_each(others, lambda k: self.share(src, sems[4], sems, k + 1).wait_send())
        self.share(src, out, sems, 0).wait()
        for_each(others, lambda k: self.away(out, sems, k + 1).wait())


class Line(Task):
    axis = "tensor"

    def remote(self, src, dst, sems, way, index):
        target = lax.axis_index("tensor") + (1 - 2 * way)
        return pltpu.make_async_remote_copy(
            src,
            dst,
            sems[0].at[way, index],
            sems[1].at[way, index],
            device_id={"tensor": target},
            device_id_type=MESH,
        )


class LineGather(Line):
    def __init__(self, block):
        self.array = block
        count = size_of("tensor")
        self.out = jax.ShapeDtypeStruct((count, *block.shape), block.dtype)
        self.sems = [
            pltpu.SemaphoreType.DMA((2, count)),
            pltpu.SemaphoreType.DMA((2, count)),
            pltpu.SemaphoreType.DMA,
        ]

    def own(self, src, out, sems):
        return pltpu.make_async_copy(src, out.at[lax.axis_index("tensor")], sems[2])

    def start(self, src, out, sems):
        me, last = lax.axis_index("tensor"), size_of("tensor") - 1
        pl.when(me < last)(lambda: self.remote(src, out.at[me], sems, 0, me).start())
        pl.when(me > 0)(lambda: self.remote(src, out.at[me], sems, 1, me).start())
        self.own(src, out, sems).start()

    def step(self, number, src, out, sems):
        me, last = lax.axis_index("tensor"), size_of("tensor") - 1
        for way, index, here, more in (
            (0, me - number, me >= number, me < last),
            (1, me + number, me + number <= last, me > 0),
        ):

            @pl.when(here)
            def _():
                copy = self.remote(out.at[index], out.at[index], sems, way, index)
                copy.wait_recv()
                pl.when(more)(copy.start)

    def finish(self, src, out, sems):
        me, last = lax.axis_index("tensor"), size_of("tensor") - 1
        for number in range(last + 1):
            for way, index, sent in (
                (0, me - number, (me >= number) & (me < last)),
                (1, me + number, (me + number <= last) & (me > 0)),
            ):
                copy = self.remote(src, out.at[me], sems, way, index)
                pl.when(sent)(copy.wait_send)
        self.own(src, out, sems).wait()


class LineSum(Line):
    place = pltpu.VMEM

    def __init__(self, blocks):
        self.array = blocks
        count = blocks.shape[0]
        self.out = jax.ShapeDtypeStruct((2, *blocks.shape[1:]), blocks.dtype)
        self.sems = [
            pltpu.SemaphoreType.DMA((2, count)),
            pltpu.SemaphoreType.DMA((2, count)),
            pltpu.VMEM((2, *blocks.shape), blocks.dtype),
        ]

    def start(self, src, out, sems):
        self.move(0, src, sems)

    def step(self, number, src, out, sems):
        if number < size_of("tensor") - 1:
            self.move(number, src, sems)

    def routes(self, number):
        me, last = lax.axis_index("tensor"), size_of("tensor") - 1
        up, down = number - me, number - (last - me)
        return (
            (0, last - up, (up >= 0) & (last - up > me), me > 0),
            (1, down, (down >= 0) & (down < me), me < last),
        )

    def move(self, number, src, sems):
        held = sems[2]
        for way, index, sends, follows in self.routes(number):

            @pl.when(sends)
            def _():
                slot = held.at[way, index]

                @pl.when(follows)
                def _():
                    self.remote(slot, slot, sems, way, index).wait_recv()
                    self.add(src, held, way, index)
                    self.remote(slot, slot, sems, way, index).start()

                @pl.when(jnp.logical_not(follows))
                def _():
                    if number > 0:
                        before = index + 1 - 2 * way
                        self.remote(slot, slot, sems, way, before).wait_send()
                    self.remote(src.at[index], slot, sems, way, index).start()

    def add(self, src, held, way, index):
        width = 2 * LANES
        for at in range(0, held.shape[3], width):
            part = held[way, index, :, at : at + width].astype(jnp.float32)
            part += src[index, :, at : at + width].astype(jnp.float32)
            held[way, index, :, at : at + width] = part.astype(held.dtype)

    def finish(self, src, out, sems):
        me, last = lax.axis_index("tensor"), size_of("tensor") - 1
        held = sems[2]
        for way, comes in ((0, me > 0), (1, me < last)):

            @pl.when(comes)
            def _():
                slot = held.at[way, me]
                self.remote(slot, slot, sems, way, me).wait_recv()
                out[way] = held[way, me]

            @pl.when(jnp.logical_not(comes))
            def _():
                out[way] = jnp.zeros(out.shape[1:], out.dtype)

        for number in range(last):
            for way, index, sends, follows in self.routes(number):
                slot = held.at[way, index]
                waits = sends if number == last - 1 else sends & follows
                pl.when(waits)(self.remote(slot, slot, sems, way, index).wait_send)


def padded_bytes(array):
    *lead, rows, columns = array.shape
    size = -(-rows // 16) * 16 * -(-columns // LANES) * LANES * array.dtype.itemsize
    for extent in lead:
        size *= extent
    return size


def held_bytes(tasks):
    total = 6 * 2**20
    for task in tasks:
        if task.place is not pl.ANY:
            total += padded_bytes(task.array) + 2 * padded_bytes(task.out)
            total += 2 * padded_bytes(task.array) if isinstance(task, LineSum) else 0
    return total


def exchange(number, *tasks):
    axes = sorted({task.axis for task in tasks})
    if "all" in axes:
        axes = ["all"]
    count = len(tasks)

    def kernel(*refs):
        sources, outs, sems = refs[:count], refs[count : 2 * count], list(refs[2 * count :])
        grouped = []
        for task in tasks:
            grouped.append([sems.pop(0) for _ in task.sems])
        barrier = pltpu.get_barrier_semaphore()

        def greet(axis, k):
            _, device = peer_at(axis, k)
            pl.semaphore_signal(barrier, inc=1, device_id=device, device_id_type=MESH)

        for axis in axes:
            for_each(size_of(axis) - 1, functools.partial(lambda a, k: greet(a, k + 1), axis))
        pl.semaphore_wait(barrier, sum(size_of(axis) - 1 for axis in axes))
        every = list(zip(tasks, sources, outs, grouped))
        for task, src, out, own in every:
            task.start(src, out, own)
        by_wait = sorted(every, key=lambda entry: isinstance(entry[0], Line))
        for step in range(1, size_of("tensor")):
            for task, src, out, own in by_wait:
                task.step(step, src, out, own)
        for task, src, out, own in every:
            task.finish(src, out, own)

    return pl.pallas_call(
        kernel,
        out_shape=[task.out for task in tasks],
        in_specs=[pl.BlockSpec(memory_space=task.place) for task in tasks],
        out_specs=[pl.BlockSpec(memory_space=task.place) for task in tasks],
        scratch_shapes=[sem for task in tasks for sem in task.sems],
        compiler_params=pltpu.CompilerParams(
            collective_id=number, has_side_effects=True, vmem_limit_bytes=held_bytes(tasks)
        ),
    )(*[task.array for task in tasks])


def spot_of(block, dim, width):
    grain = LANES if dim == block.ndim - 1 else 16
    return (dim, width) if width % grain == 0 else None


def weight_gather(block, dim):
    return PairGather(block, spot_of(block, dim, block.shape[dim]))


def joined(gathered, block, dim):
    if gathered.ndim == block.ndim:
        return gathered
    moved = jnp.moveaxis(gathered, 0, dim)
    shape = list(block.shape)
    shape[dim] *= gathered.shape[0]
    return moved.reshape(shape)


def grad_swap(term, dim):
    count = size_of("dp")
    width = term.shape[dim] // count
    low = term.astype(jnp.bfloat16)
    spot = spot_of(low, dim, width)
    if spot is None:
        shape = list(low.shape)
        shape[dim : dim + 1] = [count, width]
        low = jnp.moveaxis(low.reshape(shape), dim, 0)
    return PairSwap(low, spot)


def own_part(term, axis, dim):
    width = term.shape[dim] // size_of(axis)
    return lax.dynamic_slice_in_dim(term, my_index(axis) * width, width, dim)


def summed(own, others):
    return own + jnp.sum(others.astype(jnp.float32), axis=0)


def normalized(values):
    centred = values - jnp.mean(values, axis=-1, keepdims=True)
    spread = jnp.mean(centred * centred, axis=-1, keepdims=True)
    return centred * lax.rsqrt(spread + EPSILON)


def layer_norm(values, gain, shift):
    return normalized(values) * gain + shift


def exact_gelu(values):
    return jax.nn.gelu(values, approximate=False)


def dot(left, right, left_dim, right_dim):
    dims = (((left_dim,), (right_dim,)), ((), ()))
    return lax.dot_general(left, right, dims, preferred_element_type=jnp.float32)


def head_columns(ref, part, head, width):
    start = part * width + head * HEAD_DIM
    return ref[:, start : start + HEAD_DIM]


def attend_kernel(scale, qkv, mask, mixed, log_total):
    width = mixed.shape[1]
    for head in range(width // HEAD_DIM):
        query, keys, values = [head_columns(qkv, part, head, width) for part in range(3)]
        scores = jnp.where(mask[0:1, :] > 0, dot(query, keys, 1, 1) * scale, NEGATIVE)
        largest = jnp.max(scores, axis=-1, keepdims=True)
        powers = jnp.exp(scores - largest)
        total = jnp.sum(powers, axis=-1, keepdims=True)
        probs = (powers * (1.0 / total)).astype(jnp.bfloat16)
        columns = slice(head * HEAD_DIM, (head + 1) * HEAD_DIM)
        mixed[:, columns] = dot(probs, values, 1, 0).astype(jnp.bfloat16)
        log_total[:, head : head + 1] = largest + jnp.log(total)


def attend_back_kernel(scale, qkv, mask, log_total, grad_mixed, grads):
    width = grad_mixed.shape[1]
    for head in range(width // HEAD_DIM):
        query, keys, values = [head_columns(qkv, part, head, width) for part in range(3)]
        grad = head_columns(grad_mixed, 0, head, width)
        scores = jnp.where(mask[0:1, :] > 0, dot(query, keys, 1, 1) * scale, NEGATIVE)
        probs = jnp.exp(scores - log_total[:, head : head + 1])
        grad_probs = dot(grad, values, 1, 1)
        inner = jnp.sum(grad_probs * probs, axis=-1, keepdims=True)
        grad_scores = (probs * (grad_probs - inner)).astype(jnp.bfloat16)
        results = (
            dot(grad_scores, keys, 1, 0) * scale,
            dot(grad_scores, query, 0, 0) * scale,
            dot(probs.astype(jnp.bfloat16), grad, 0, 0),
        )
        for part, result in enumerate(results):
            start = part * width + head * HEAD_DIM
            grads[:, start : start + HEAD_DIM] = result.astype(jnp.bfloat16)


def in_vmem(kernel, outs, *arrays):
    return pl.pallas_call(
        kernel,
        out_shape=outs,
        in_specs=[pl.BlockSpec(memory_space=pltpu.VMEM)] * len(arrays),
        out_specs=[pl.BlockSpec(memory_space=pltpu.VMEM)] * len(outs),
        compiler_params=pltpu.CompilerParams(vmem_limit_bytes=32 * 2**20),
    )(*arrays)


def row_validity(counts, seq, rows):
    places = jnp.arange(rows, dtype=jnp.int32)
    owner = places // seq
    position = places - owner * seq
    picks = owner[:, None] == jnp.arange(counts.shape[0], dtype=jnp.int32)[None, :]
    return position < jnp.sum(jnp.where(picks, counts[None, :], 0), axis=1)


def row_sum(part, rows):
    return LineSum(part.astype(jnp.bfloat16).reshape(-1, rows, part.shape[1]))


def row_permutes(part, rows):
    count = size_of("tensor")
    parts = part.reshape(count, rows, part.shape[1])
    others = []
    for k in range(1, count):
        index, _ = peer_at("tensor", k)
        block = lax.dynamic_index_in_dim(parts, index, 0, keepdims=False)
        pairs = [(i, (i + k) % count) for i in range(count)]
        others.append(lax.ppermute(block, "tensor", pairs))
    return others


def on_device(tokens, counts, vectors, fc1_bias, w_qkv, w_out, w_fc1, w_fc2, cotangent):
    tensor_count = lax.axis_size("tensor")
    tensor_index = lax.axis_index("tensor")
    devices = size_of("all")
    model_width = tokens.shape[1]
    vector_size = vectors.size
    small_size = vector_size + fc1_bias.size
    small_rows = -(-small_size // (8 * LANES)) * 8
    small = jnp.concatenate([vectors.reshape(-1), fc1_bias])
    small = jnp.pad(small, (0, small_rows * LANES - small_size)).reshape(small_rows, LANES)
    local_rows = tokens.shape[0]
    block_rows = local_rows * tensor_count
    images = counts.shape[0]
    local_valid = row_validity(counts, block_rows // images, block_rows)
    local_valid = lax.dynamic_slice_in_dim(local_valid, tensor_index * local_rows, local_rows)
    local_valid = local_valid.astype(jnp.float32)[:, None]
    masked_out = local_valid * cotangent
    width = w_qkv.shape[2]
    w_qkv_flat = w_qkv.transpose(1, 0, 2).reshape(w_qkv.shape[1], 3 * width)
    small_all, unscaled, gathered_grad, qkv_all, out_all = exchange(
        0,
        Gather("all", small),
        LineGather(normalized(tokens).astype(jnp.bfloat16)),
        LineGather(masked_out.astype(jnp.bfloat16)),
        weight_gather(w_qkv_flat, 0),
        weight_gather(w_out, 1),
    )
    qkv_all = joined(qkv_all, w_qkv_flat, 0)
    out_all = joined(out_all, w_out, 1)
    small_all = small_all.reshape(devices, small_rows * LANES)
    full_vectors = small_all[:, :vector_size].reshape(devices, vectors.shape[0], -1)
    full_vectors = full_vectors.transpose(1, 0, 2).reshape(vectors.shape[0], model_width)
    full_fc1 = small_all[:, vector_size:small_size].reshape(-1)
    gathered_grad = gathered_grad.reshape(block_rows, model_width)
    unscaled = unscaled.reshape(block_rows, model_width).astype(jnp.float32)
    gathered = (unscaled * full_vectors[0] + full_vectors[1]).astype(jnp.bfloat16)
    seq = block_rows // images
    hidden_width = w_fc1.shape[1]
    heads_local = width // HEAD_DIM
    scale = HEAD_DIM ** (-0.5)
    block_valid = row_validity(counts, seq, block_rows)
    query_bias = lax.dynamic_slice_in_dim(full_vectors[2], tensor_index * width, width)
    value_bias = lax.dynamic_slice_in_dim(full_vectors[3], tensor_index * width, width)
    hidden_bias = lax.dynamic_slice_in_dim(full_fc1, tensor_index * hidden_width, hidden_width)
    qkv_bias = jnp.concatenate([query_bias, jnp.zeros_like(query_bias), value_bias])
    projected = jnp.dot(gathered, qkv_all, preferred_element_type=jnp.float32)
    qkv = (projected + qkv_bias).astype(jnp.bfloat16)
    mask = jnp.broadcast_to(block_valid.astype(jnp.float32), (8, block_rows))
    mixed_all, log_total = in_vmem(
        functools.partial(attend_kernel, scale),
        [
            jax.ShapeDtypeStruct((block_rows, width), jnp.bfloat16),
            jax.ShapeDtypeStruct((block_rows, heads_local), jnp.float32),
        ],
        qkv,
        mask,
    )
    attn_part = jnp.dot(mixed_all, out_all, preferred_element_type=jnp.float32)
    attn_low = attn_part.astype(jnp.bfloat16).reshape(-1, local_rows, model_width)
    attn_others, fc1_all, fc2_all = exchange(
        1, Swap("tensor", attn_low), weight_gather(w_fc1, 0), weight_gather(w_fc2, 1)
    )
    fc1_all = joined(fc1_all, w_fc1, 0)
    fc2_all = joined(fc2_all, w_fc2, 1)
    attn_local = summed(own_part(attn_part, "tensor", 0), attn_others)
    middle = tokens + local_valid * (attn_local + full_vectors[4])
    normed2 = layer_norm(middle, full_vectors[5], full_vectors[6]).astype(jnp.bfloat16)
    (gathered2,) = exchange(2, LineGather(normed2))
    gathered2 = gathered2.reshape(block_rows, model_width)
    pre = jnp.dot(gathered2, fc1_all, preferred_element_type=jnp.float32) + hidden_bias
    hidden_float, gelu_back = jax.vjp(exact_gelu, pre)
    hidden = hidden_float.astype(jnp.bfloat16)
    mlp_part = jnp.dot(hidden, fc2_all, preferred_element_type=jnp.float32)
    grad_shift2 = jnp.sum(masked_out, axis=0)
    fc2_term = jnp.einsum("rf,rd->fd", hidden, gathered_grad, preferred_element_type=jnp.float32)
    grad_hidden = jnp.einsum(
        "rd,fd->rf", gathered_grad, fc2_all, preferred_element_type=jnp.float32
    )
    grad_pre = gelu_back(grad_hidden)[0].astype(jnp.bfloat16)
    hidden_bias_grad = jnp.sum(grad_pre.astype(jnp.float32), axis=0)
    fc1_term = jnp.einsum("rd,rf->df", gathered2, grad_pre, preferred_element_type=jnp.float32)
    normed2_part = jnp.einsum("rf,df->rd", grad_pre, fc1_all, preferred_element_type=jnp.float32)
    normed2_others, fc2_others = exchange(
        3, row_sum(normed2_part, local_rows), grad_swap(fc2_term, 1)
    )
    grad_normed2 = summed(own_part(normed2_part, "tensor", 0), normed2_others)
    fc2_grad = summed(own_part(fc2_term, "dp", 1), fc2_others)
    second_norm, second_back = jax.vjp(layer_norm, middle, full_vectors[5], full_vectors[6])
    grad_through, gain2_grad, shift2_grad = second_back(grad_normed2)
    grad_middle = cotangent + grad_through
    masked_middle = local_valid * grad_middle
    out_bias_grad = jnp.sum(masked_middle, axis=0)
    gathered_attn, fc1_others = exchange(
        4, LineGather(masked_middle.astype(jnp.bfloat16)), grad_swap(fc1_term, 0)
    )
    fc1_grad = summed(own_part(fc1_term, "dp", 0), fc1_others)
    gathered_attn, mlp_low = lax.optimization_barrier(
        (gathered_attn, mlp_part.astype(jnp.bfloat16))
    )
    mlp_others = row_permutes(mlp_low, local_rows)
    mlp_local = own_part(mlp_part, "tensor", 0)
    for block in mlp_others:
        mlp_local = mlp_local + block.astype(jnp.float32)
    layer_out = middle + local_valid * (mlp_local + full_vectors[7])
    gathered_attn = gathered_attn.reshape(block_rows, model_width)
    out_term = jnp.einsum("re,rd->ed", mixed_all, gathered_attn, preferred_element_type=jnp.float32)
    grad_mixed = jnp.einsum("rd,ed->re", gathered_attn, out_all, preferred_element_type=jnp.float32)
    (qkv_back,) = in_vmem(
        functools.partial(attend_back_kernel, scale),
        [jax.ShapeDtypeStruct(qkv.shape, jnp.bfloat16)],
        qkv,
        mask,
        log_total,
        grad_mixed.astype(jnp.bfloat16),
    )
    qkv_bias_grad = jnp.sum(qkv_back.astype(jnp.float32), axis=0)
    query_bias_grad, value_bias_grad = qkv_bias_grad[:width], qkv_bias_grad[2 * width :]
    qkv_term = jnp.einsum("rd,re->de", gathered, qkv_back, preferred_element_type=jnp.float32)
    normed_part = jnp.einsum("re,de->rd", qkv_back, qkv_all, preferred_element_type=jnp.float32)
    gain1_grad = jnp.sum(normed_part * unscaled, axis=0)
    shift1_grad = jnp.sum(normed_part, axis=0)
    zeros_model = jnp.zeros((model_width,), jnp.float32)
    query_bias_full = lax.dynamic_update_slice_in_dim(
        zeros_model, query_bias_grad, tensor_index * width, 0
    )
    value_bias_full = lax.dynamic_update_slice_in_dim(
        zeros_model, value_bias_grad, tensor_index * width, 0
    )
    vector_terms = jnp.stack(
        [
            gain1_grad,
            shift1_grad,
            query_bias_full,
            value_bias_full,
            out_bias_grad,
            gain2_grad,
            shift2_grad,
            grad_shift2,
        ]
    )
    zeros_hidden = jnp.zeros((full_fc1.shape[0],), jnp.float32)
    hidden_bias_full = lax.dynamic_update_slice_in_dim(
        zeros_hidden, hidden_bias_grad, tensor_index * hidden_width, 0
    )
    vector_blocks = vector_terms.reshape(vectors.shape[0], devices, -1).transpose(1, 0, 2)
    small_terms = jnp.concatenate(
        [vector_blocks.reshape(devices, -1), hidden_bias_full.reshape(devices, -1)], axis=1
    )
    small_terms = jnp.pad(small_terms, ((0, 0), (0, small_rows * LANES - small_size)))
    small_terms = small_terms.reshape(devices, small_rows, LANES)
    normed_others, qkv_others, out_others, small_others = exchange(
        5,
        row_sum(normed_part, local_rows),
        grad_swap(qkv_term, 0),
        grad_swap(out_term, 1),
        Swap("all", small_terms),
    )
    grad_normed = summed(own_part(normed_part, "tensor", 0), normed_others)
    qkv_grad = summed(own_part(qkv_term, "dp", 0), qkv_others)
    qkv_grad = qkv_grad.reshape(-1, 3, width).transpose(1, 0, 2)
    out_grad = summed(own_part(out_term, "dp", 1), out_others)
    first_norm, first_back = jax.vjp(layer_norm, tokens, full_vectors[0], full_vectors[1])
    grad_input_norm, _, _ = first_back(grad_normed)
    input_grad = grad_middle + grad_input_norm
    small_grad = summed(own_part(small_terms, "all", 0)[0], small_others).reshape(-1)
    vectors_grad = small_grad[:vector_size].reshape(vectors.shape)
    fc1_bias_grad = small_grad[vector_size:small_size]
    return (
        layer_out,
        input_grad,
        vectors_grad,
        fc1_bias_grad,
        qkv_grad,
        out_grad,
        fc1_grad,
        fc2_grad,
    )


def solution(mesh):
    placed = (
        P(("dp", "tensor"), None),
        P("dp"),
        P(None, ("dp", "tensor")),
        P(("dp", "tensor")),
        P(None, "dp", "tensor"),
        P("tensor", "dp"),
        P("dp", "tensor"),
        P("tensor", "dp"),
        P(("dp", "tensor"), None),
    )
    return jax.shard_map(
        on_device,
        mesh=mesh,
        in_specs=placed,
        out_specs=(
            P(("dp", "tensor"), None),
            P(("dp", "tensor"), None),
            P(None, ("dp", "tensor")),
            P(("dp", "tensor")),
            P(None, "dp", "tensor"),
            P("tensor", "dp"),
            P("dp", "tensor"),
            P("tensor", "dp"),
        ),
        check_vma=False,
    )
```
